256 devices in a mesh: sub: 128 (over z, y, x_hi, core), lm: 2 (over x_lo).
Axes of the slice: x: 4 (x_hi: 2, x_lo: 2; x = x_hi * 2 + x_lo), y: 4, z: 8, core: 2. Of those that a mesh axis runs over, the one named last changes fastest.
Arguments:
- jacobian: bfloat16 [128, 8, 384, 128], P('sub', 'lm'), may hold values from -0.30618622 to 0.30618622
- camera_block: int32 [128, 8], P('sub', 'lm'), may hold values from 0 to 8
- landmark_block: int32 [128, 8], P('sub', 'lm'), may hold values from 9 to 17
Outputs:
- factors: float32 [3, 256, 252, 576], P(None, ('sub', 'lm'))
- top_front: float32 [2, 256, 36, 1152], P(None, ('sub', 'lm'))
The draws below stay inside these ranges and needn't reach their ends.
Inputs may be any that keep to these rules, and one draw needn't show every extreme that they name: `camera_block`: camera parts lie in the first half of a front's unknowns. `landmark_block`: landmark parts lie in the second half of a front's unknowns.
All inputs are finite; a program needn't handle non-finite values.
Results may differ from the reference program's by a relative error of at most 0.0003.
Values may be sent and summed in bfloat16 or wider, within the bound.
A program may use at most 64 MiB of HBM per device.

```python
import jax
import jax.numpy as jnp
from jax import lax

JR = 384
BW = 64
F = 1152
LEVELS = 3
E = 576
BLOCKS = 8
SUBMAPS = 128
N_LM = 2


def draw_jacobian(key, part):
    shape = (SUBMAPS, BLOCKS, JR, BW)
    first_key = jax.random.fold_in(key, 11)
    second_key = jax.random.fold_in(key, 23)
    camera_cols = jnp.clip(jax.random.normal(first_key, shape, jnp.float32), -3.3, 3.3)
    noise_cols = jnp.clip(jax.random.normal(second_key, shape, jnp.float32), -3.3, 3.3)
    landmark_cols = 0.8 * camera_cols + 0.6 * noise_cols
    scale_value = JR ** (-0.5)
    return (jnp.concatenate([camera_cols, landmark_cols], axis=3) * scale_value).astype(jnp.bfloat16)


def touch_ends(values, key, smallest, high):
    spot = [jax.random.randint(jax.random.fold_in(key, axis), (), 0, length) for axis, length in enumerate(values.shape)]
    widest = values.shape.index(max(values.shape))
    next_to = spot[:widest] + [(spot[widest] + 1) % values.shape[widest]] + spot[widest + 1:]
    return values.at[tuple(spot)].set(smallest).at[tuple(next_to)].set(high)


def setup_inputs(seed: int = 0) -> dict:
    streams_of = jax.random.split(jax.random.key(seed), 4)
    return {
        "jacobian": draw_jacobian(jax.random.fold_in(streams_of[3], 71), 0),
        "camera_block": touch_ends(jax.random.randint(streams_of[1], (SUBMAPS, BLOCKS), 0, F // (2 * BW)), jax.random.fold_in(streams_of[1], 1), 0, (F // (2 * BW)) - 1).astype(jnp.int32),
        "landmark_block": touch_ends(jax.random.randint(streams_of[2], (SUBMAPS, BLOCKS), F // (2 * BW), F // BW), jax.random.fold_in(streams_of[2], 1), F // (2 * BW), (F // BW) - 1).astype(jnp.int32),
    }


damping_value = 1.0

def assemble(blocks, cameras, landmarks):
    block_count = blocks.shape[0]
    widened = blocks.astype(jnp.float32)
    tiles = jnp.einsum('nrc,nrd->ncd', widened, widened, precision=lax.Precision.HIGHEST)
    tiles = tiles.reshape(block_count, 2, BW, 2, BW).transpose(0, 1, 3, 2, 4)
    indices = jnp.stack([cameras, landmarks], axis=1)
    nblocks = F // BW
    blocked = jnp.zeros((nblocks, nblocks, BW, BW), jnp.float32)
    for first in range(2):
        for second in range(2):
            blocked = blocked.at[indices[:, first], indices[:, second]].add(tiles[:, first, second])
    whole_front = blocked.transpose(0, 2, 1, 3).reshape(F, F)
    return whole_front + damping_value * jnp.eye(F, dtype=jnp.float32)

def merge(lower_child, upper_child):
    shared = lower_child[:E, :E] + upper_child[:E, :E]
    diag_factor = jnp.linalg.cholesky(shared)
    coupled = jnp.concatenate([lower_child[E:, :E], upper_child[E:, :E]], axis=0)
    coupling = jax.scipy.linalg.solve_triangular(diag_factor, coupled.T, lower=True).T
    blank = jnp.zeros((E, E), jnp.float32)
    private = jnp.concatenate([jnp.concatenate([lower_child[E:, E:], blank], axis=1), jnp.concatenate([blank, upper_child[E:, E:]], axis=1)], axis=0)
    parent = private - jnp.dot(coupling, coupling.T, precision=lax.Precision.HIGHEST)
    return (diag_factor, coupling, parent)

def cyclic_rows(stacked, spread):
    groups = stacked.shape[0]
    blocks = stacked.shape[1]
    width = stacked.shape[3]
    grouped = stacked.reshape(groups, blocks, E // spread, spread, width)
    return grouped.transpose(1, 0, 3, 2, 4).reshape(blocks, groups * spread, E // spread, width)

def reference(jacobian, camera_block, landmark_block):
    fronts = jax.vmap(assemble)(jacobian, camera_block, landmark_block)
    collected = []
    for depth_level in range(LEVELS):
        diag_factor, coupling, fronts = jax.vmap(merge)(fronts[0::2], fronts[1::2])
        stacked = jnp.concatenate([diag_factor[:, None], coupling.reshape(-1, 2, E, E)], axis=1)
        collected.append(cyclic_rows(stacked, 2 ** (depth_level + 1) * N_LM))
    top_front = cyclic_rows(fronts.reshape(-1, 2, E, F), 2 ** LEVELS * N_LM)
    return (jnp.concatenate(collected, axis=2), top_front)
```

```python
import jax
import jax.numpy as jnp
from jax import lax
from jax.experimental import pallas as pl
from jax.experimental.pallas import tpu as pltpu
from jax.sharding import PartitionSpec as P

BW = 64
E = 576
NB = E // BW
EP = 640
WIDE = 3 * EP
PEERS = 16
MESH = pl.DeviceIdType.MESH
f32 = jnp.float32
bf16 = jnp.bfloat16


def lane_ids(shape):
    return lax.broadcasted_iota(jnp.int32, shape, 1)


def row_ids(shape):
    return lax.broadcasted_iota(jnp.int32, shape, 0)


def over_lanes(tile, column):
    return jnp.broadcast_to(tile[:, column : column + 1], tile.shape)


def over_rows(tile, row):
    return jnp.broadcast_to(tile[row : row + 1, :], tile.shape)


def factor_blocks(blocks):
    sub = row_ids((8, 128))
    mats = [[block[8 * i : 8 * i + 8, :] for i in range(8)] for block in blocks]
    for s in range(8):
        cols = [[[over_lanes(m[i], 8 * s + t) for i in range(s, 8)] for t in range(8)] for m in mats]
        pivots = [jnp.zeros((8, 128), f32) for _ in mats]
        for t in range(8):
            for b, m in enumerate(mats):
                row = over_rows(m[s], t)
                pivot = over_rows(cols[b][t][0], t)
                inverse = 1.0 / pivot
                pivots[b] = jnp.where(sub == t, pivot, pivots[b])
                scaled = [c * inverse for c in cols[b][t]]
                scaled[0] = jnp.where(sub > t, scaled[0], 0.0)
                for i in range(s, 8):
                    m[i] = m[i] - scaled[i - s] * row
                for u in range(t + 1, 8):
                    across = over_rows(cols[b][u][0], t)
                    for i in range(8 - s):
                        cols[b][u][i] = cols[b][u][i] - scaled[i] * across
        for b, m in enumerate(mats):
            m[s] = m[s] * lax.rsqrt(pivots[b])
    return [jnp.concatenate(m, axis=0) for m in mats]


def halves(value):
    high = value.astype(bf16)
    return high, (value - high.astype(f32)).astype(bf16)


def left_parts(value):
    high = value.astype(bf16).astype(f32)
    both = jnp.concatenate([high, value - high], axis=1).astype(bf16)
    return jnp.concatenate([both, high.astype(bf16)], axis=1)


def right_lanes(value):
    high = value.astype(bf16).astype(f32)
    both = jnp.concatenate([high, high], axis=1).astype(bf16)
    return jnp.concatenate([both, (value - high).astype(bf16)], axis=1)


def right_parts(value):
    high, low = halves(value)
    return jnp.concatenate([high, high, low], axis=0)


def mm(left, right):
    return jnp.dot(left, right, preferred_element_type=f32)


def mm_nt(left, right):
    return lax.dot_general(left, right, (((1,), (1,)), ((), ())), preferred_element_type=f32)


def group_place():
    return (lax.axis_index("sub") % 8) * 2 + lax.axis_index("lm")


def peer(mask):
    sub, lm = lax.axis_index("sub"), lax.axis_index("lm")
    step = mask // 2
    for bit in (1, 2, 4):
        if step & bit:
            sub = sub + bit - 2 * bit * ((sub // bit) % 2)
    if mask & 1:
        lm = 1 - lm
    return (sub, lm)


def relative(place, mask):
    for bit in (1, 2, 4, 8):
        if mask & bit:
            place = place + bit - 2 * bit * ((place // bit) % 2)
    return place


def greet(masks):
    barrier = pltpu.get_barrier_semaphore()
    for mask in masks:
        pl.semaphore_signal(barrier, inc=1, device_id=peer(mask), device_id_type=MESH)
    pl.semaphore_wait(barrier, len(masks))


def trade_kernel(cam_ref, ids_ref, cams_ref, allids_ref, send, recv, id_send, id_recv):
    place = group_place()
    greet(range(1, PEERS))
    copies = []
    for mask in (3, 1, 2):
        copies.append(
            pltpu.make_async_remote_copy(
                cam_ref, cams_ref.at[place % 4], send.at[mask], recv.at[mask], device_id=peer(mask), device_id_type=MESH
            )
        )
    for mask in range(1, PEERS):
        copies.append(
            pltpu.make_async_remote_copy(
                ids_ref, allids_ref.at[place], id_send.at[mask], id_recv.at[mask], device_id=peer(mask), device_id_type=MESH
            )
        )
    for copy in copies:
        copy.start()
    cams_ref[pl.ds(place % 4, 1)] = cam_ref[...][None]
    allids_ref[pl.ds(place, 1)] = ids_ref[...][None]
    for copy in copies:
        copy.wait()


ACROSS = (12, 13, 8, 9, 4, 5, 1)


def gather_kernel(own_ref, all_ref, send, recv, pass_send):
    place = group_place()
    greet(ACROSS + (2,))

    def sending(mask):
        return pltpu.make_async_remote_copy(
            own_ref, all_ref.at[place], send.at[mask], recv.at[mask], device_id=peer(mask), device_id_type=MESH
        )

    firsts = {mask: sending(mask) for mask in ACROSS + (2,)}
    for mask in ACROSS + (2,):
        firsts[mask].start()
    all_ref[pl.ds(place, 1)] = own_ref[...][None]
    passed = []
    for mask in ACROSS[::-1]:
        firsts[mask].wait_recv()
        slot = all_ref.at[relative(place, mask)]
        copy = pltpu.make_async_remote_copy(
            slot, slot, pass_send.at[mask], recv.at[mask ^ 2], device_id=peer(2), device_id_type=MESH
        )
        copy.start()
        passed.append(copy)
    firsts[2].wait_recv()
    for copy in passed:
        copy.wait()
    for mask in ACROSS + (2,):
        firsts[mask].wait_send()


def eliminate_cameras_kernel(cam_ref, cams_ref, tiles_ref, own_ref, packet_ref, factor_ref, total):
    lane = lane_ids((BW, 128))
    row = row_ids((BW, 128))
    start = jnp.where(lane == row, 2.0, jnp.where(lane == row + BW, 1.0, 0.0)).astype(f32)
    for c in range(NB):
        total[c] = start
    for j in range(16):
        packed = cams_ref[j // 4, (j % 4) // 2]
        if j % 2:
            packed = pltpu.roll(packed, BW, 1)
        c = cam_ref[j]
        total[c] = total[c] + jnp.where(lane < BW, packed, 0.0)

    def three(step, carry):
        done = factor_blocks([total[3 * step + b] for b in range(3)])
        for b in range(3):
            factor_ref[3 * step + b] = done[b]
        return carry

    lax.fori_loop(0, 3, three, 0)
    for b in range(4):
        tile = tiles_ref[b]
        inverse = pltpu.roll(factor_ref[own_ref[b]], BW, 1)[:, :BW]
        right = jnp.concatenate([right_lanes(inverse), jnp.zeros((BW, 192), bf16)], axis=0)
        solved = mm_nt(left_parts(tile[:, :BW]), right)
        packet_ref[b] = jnp.where(lane < BW, solved, tile)


def eliminate(fronts, own=None):
    lane = lane_ids((BW, 128))
    row = row_ids((BW, 128))
    unit = jnp.where(lane == row + BW, 1.0, 0.0).astype(f32)
    diag = [front[0:BW, 0:128] for front in fronts]
    for k in range(NB):
        r0, t0 = BW * k, k // 2 * 128
        r1, t1 = r0 + BW, (k + 1) // 2 * 128
        if k % 2:
            diag = [pltpu.roll(tile, BW, 1) for tile in diag]
        done = factor_blocks([jnp.where(lane < BW, tile, unit) for tile in diag])
        following = []
        for front, block in zip(fronts, done):
            inverse = pltpu.roll(block, BW, 1)[:, :BW]
            upper = mm(left_parts(inverse), right_parts(front[r0:r1, t0:WIDE]))
            corner = jnp.where(jnp.logical_and(lane >= row, lane < BW), block, 0.0)
            if k % 2:
                first = pltpu.roll(corner, BW, 1)
            else:
                first = jnp.where(lane < BW, corner, upper[:, :128])
            front[r0:r1, t0:t0 + 128] = first
            front[r0:r1, t0 + 128:WIDE] = upper[:, 128:]
            high, low = halves(upper)
            parts = jnp.concatenate([high, high, low], axis=0)
            left = None
            if k < NB - 1:
                turned = upper[:, t1 - t0:EP - t0].T
                left = left_parts(turned[r1 - t1:E - t1])
                following.append(front[r1:r1 + BW, t1:t1 + 128] - mm(left[:BW], parts[:, t1 - t0:t1 - t0 + 128]))
            if own is not None:
                block_lanes = own[:, r0:r1]
                own_solved = mm_nt(left_parts(block_lanes), right_lanes(inverse))
                own_left = left_parts(own_solved)
            begin = t1 if k < NB - 1 else EP
            bounds = [n for n in (0, 256, 512, 640, 896, 1152, 1408, 1664, 1920) if n > begin]
            for n1 in bounds:
                n0 = begin
                begin = n1
                last = min(E, n1)
                piece = parts[:, n0 - t0:n1 - t0]
                if left is not None:
                    front[r1:last, n0:n1] = front[r1:last, n0:n1] - mm(left[:last - r1], piece)
                if own is not None:
                    own[:, n0:n1] = own[:, n0:n1] - mm(own_left, piece)
            if own is not None:
                own[:, r0:r1] = own_solved
        diag = following


def climb_kernel(
    place_ref, cam_ref, lmk_ref, packet_ref, factor_ref, out_ref, top_ref,
    front, upper_front, private, spread, spread_high, spread_low, rows21, rows11, left_all, own,
):
    place = place_ref[0]
    lane = lane_ids((BW, 128))
    row = row_ids((BW, 128))
    zero_tile = jnp.zeros((BW, 128), f32)

    def clear(ref, count, width):
        def step(i, carry):
            ref[pl.ds(pl.multiple_of(i * BW, BW), BW), :] = jnp.zeros((BW, width), f32)
            return carry

        lax.fori_loop(0, count // BW, step, 0)

    for g in range(2):
        clear(front.at[g], EP, WIDE)
    for m in range(4):
        for n in range(5):
            clear(private.at[m, n], EP, 128)
    clear(upper_front, EP, WIDE)
    for n in range(5):
        clear(rows21.at[0, n], 2 * EP, 128)
        clear(rows11.at[n], EP, 128)
    own[...] = jnp.zeros(own.shape, f32)
    for i in range(NB):
        spot = jnp.where(lane == row + BW * (i % 2), 1.0, 0.0).astype(f32)
        tile = (slice(BW * i, BW * i + BW), slice(i // 2 * 128, i // 2 * 128 + 128))
        for g in range(2):
            front[(g,) + tile] = 2.0 * spot
        for m in range(4):
            private[m, i // 2, BW * i:BW * i + BW, :] = spot

    pair = place // 4
    for b in range(16):
        j = pair * 16 + b
        c, l = cam_ref[j], lmk_ref[j]
        packet = packet_ref[j]
        side = c % 2
        both = jnp.where(lane < BW, packet, pltpu.roll(packet, BW, 1))
        placed = jnp.where(lane // BW == side, both, 0.0)
        spot = (0, c // 2, pl.ds(pl.multiple_of(b // 8 * EP + l * BW, BW), BW), slice(None))
        rows21[spot] = rows21[spot] + placed
    for c in range(NB):
        turned = factor_ref[c].T[:BW]
        keep = lane_ids((BW, BW)) <= row_ids((BW, BW))
        rows11[c // 2, BW * c:BW * c + BW, c % 2 * BW:c % 2 * BW + BW] = jnp.where(keep, turned, 0.0)
    place0 = place % 4
    for n in range(0, EP, 128):
        wide = min(128, E - n)
        out_ref[0, 0:144, n:n + wide] = rows11[n // 128, pl.ds(place0, 144, stride=4), :][:, :wide]
        out_ref[1, 0:144, n:n + wide] = rows21[0, n // 128, pl.ds(place0, 144, stride=4), :][:, :wide]
        out_ref[2, 0:144, n:n + wide] = rows21[0, n // 128, pl.ds(EP + place0, 144, stride=4), :][:, :wide]

    for m in range(4):
        g, h = m // 2, m % 2

        def clear_spread(c, carry):
            spread[c] = jnp.zeros((BW, 2 * EP), f32)
            return carry

        lax.fori_loop(0, NB, clear_spread, 0)
        for b in range(16):
            j = 16 * m + b
            c, l = cam_ref[j], lmk_ref[j]
            packet = packet_ref[j]
            side = l % 2
            across = packet.T[:BW]
            both = jnp.concatenate([across, across], axis=1)
            placed = jnp.where(lane // BW == side, both, 0.0)
            spot = (c, slice(None), pl.ds(pl.multiple_of(b // 8 * EP + l // 2 * 128, 128), 128))
            spread[spot] = spread[spot] + placed
            squares = jnp.where(lane >= BW, packet, pltpu.roll(packet, BW, 1))
            squares = jnp.where(lane // BW == side, squares, 0.0)
            rows = pl.ds(pl.multiple_of(l * BW, BW), BW)
            if b < 8:
                spot = (g, rows, pl.ds(pl.multiple_of(l // 2 * 128, 128), 128))
                front[spot] = front[spot] + squares
            else:
                spot = (m, l // 2, rows, slice(None))
                private[spot] = private[spot] + squares

        def split_spread(c, carry):
            high, low = halves(spread[c])
            spread_high[c] = high
            spread_low[c] = low
            return carry

        lax.fori_loop(0, NB, split_spread, 0)
        for b in range(16):
            j = 16 * m + b
            c, l = cam_ref[j], lmk_ref[j]
            left = left_parts(packet_ref[j][:, :BW])
            rows = pl.ds(pl.multiple_of(l * BW, BW), BW)
            begin = 0 if b < 8 else EP
            high = spread_high[c, :, begin:]
            taken = mm(left, jnp.concatenate([high, high, spread_low[c, :, begin:]], axis=0))
            if b < 8:
                front[g, rows, 0:EP] = front[g, rows, 0:EP] - taken[:, :EP]
                front[g, rows, EP * (1 + h):EP * (2 + h)] = front[g, rows, EP * (1 + h):EP * (2 + h)] - taken[:, EP:]
            else:
                for n in range(5):
                    private[m, n, rows, :] = private[m, n, rows, :] - taken[:, 128 * n:128 * n + 128]

    eliminate([front.at[0], front.at[1]])
    place1 = place % 8
    mine = place // 8
    for g in range(2):
        for j in range(5):
            for i in range(10):
                rows21[g, j, 128 * i:128 * i + 128, :] = front[
                    g, 128 * j:128 * j + 128, EP + 128 * i:EP + 128 * i + 128
                ].T
    for j in range(5):
        for i in range(j, 5):
            rows11[j, 128 * i:128 * i + 128, :] = front[
                mine, 128 * j:128 * j + 128, 128 * i:128 * i + 128
            ].T
        for i in range(j):
            rows11[j, 128 * i:128 * i + 128, :] = jnp.zeros((128, 128), f32)
    for n in range(0, EP, 128):
        wide = min(128, E - n)
        out_ref[0, 144:216, n:n + wide] = rows11[n // 128, pl.ds(place1, 72, stride=8), :][:, :wide]
        out_ref[1, 144:216, n:n + wide] = rows21[mine, n // 128, pl.ds(place1, 72, stride=8), :][:, :wide]
        out_ref[2, 144:216, n:n + wide] = rows21[mine, n // 128, pl.ds(EP + place1, 72, stride=8), :][:, :wide]
    for g in range(2):
        for n in range(0, EP, 128):
            high, low = halves(rows21[g, n // 128, 0:E, :])
            left_all[g, 0:E, n:n + 128] = high
            left_all[g, 0:E, EP + n:EP + n + 128] = low
            left_all[g, 0:E, 2 * EP + n:2 * EP + n + 128] = high
            few = rows21[g, n // 128, pl.ds(EP + place, 40, stride=16), :]
            high, low = halves(jnp.concatenate([few, jnp.zeros((24, 128), f32)], axis=0))
            left_all[g, E:EP, n:n + 128] = high
            left_all[g, E:EP, EP + n:EP + n + 128] = low
            left_all[g, E:EP, 2 * EP + n:2 * EP + n + 128] = high
        for n0, n1 in ((0, 256), (256, 512), (512, 640), (640, 896), (896, 1152), (1152, 1280)):
            high, low = halves(front[g, :, EP + n0:EP + n1])
            taken = mm(left_all[g], jnp.concatenate([high, high, low], axis=0))
            if n0 < EP:
                base = jnp.concatenate([private[2 * g, n // 128, 0:E, :] for n in range(n0, n1, 128)], axis=1) - taken[:E]
                if g:
                    base = base + upper_front[0:E, n0:n1]
                upper_front[0:E, n0:n1] = base
                own[40 * g:40 * g + 40, n0:n1] = -taken[E:E + 40]
            else:
                shift = EP * g
                upper_front[0:E, n0 + shift:n1 + shift] = -taken[:E]
                for n in range(n0, n1, 128):
                    kept = private[2 * g + 1, (n - EP) // 128, pl.ds(place, 40, stride=16), :]
                    own[40 * g:40 * g + 40, n + shift:n + shift + 128] = kept - taken[E:E + 40, n - n0:n - n0 + 128]

    eliminate([upper_front], own)
    for j in range(5):
        for i in range(j, 5):
            rows11[j, 128 * i:128 * i + 128, :] = upper_front[
                128 * j:128 * j + 128, 128 * i:128 * i + 128
            ].T
    for n in range(0, EP, 128):
        wide = min(128, E - n)
        out_ref[0, 216:252, n:n + wide] = rows11[n // 128, pl.ds(place, 36, stride=16), :][:, :wide]
    for h in range(2):
        out_ref[1 + h, 216:252, :] = own[40 * h:40 * h + 36, 0:E]
        top_ref[h, :, 0:E] = own[40 * h:40 * h + 36, EP:EP + E]
        top_ref[h, :, E:2 * E] = own[40 * h:40 * h + 36, 2 * EP:2 * EP + E]


VMEM = pl.BlockSpec(memory_space=pltpu.VMEM)
SMEM = pl.BlockSpec(memory_space=pltpu.SMEM)


def climb(place, cameras, landmarks, packets, factors):
    return pl.pallas_call(
        climb_kernel,
        out_shape=(jax.ShapeDtypeStruct((3, 252, E), f32), jax.ShapeDtypeStruct((2, 36, 2 * E), f32)),
        in_specs=[SMEM, SMEM, SMEM, VMEM, VMEM],
        out_specs=(VMEM, VMEM),
        scratch_shapes=[
            pltpu.VMEM((2, EP, WIDE), f32),
            pltpu.VMEM((EP, WIDE), f32),
            pltpu.VMEM((4, 5, EP, 128), f32),
            pltpu.VMEM((NB, BW, 2 * EP), f32),
            pltpu.VMEM((NB, BW, 2 * EP), bf16),
            pltpu.VMEM((NB, BW, 2 * EP), bf16),
            pltpu.VMEM((2, 5, 2 * EP, 128), f32),
            pltpu.VMEM((5, EP, 128), f32),
            pltpu.VMEM((2, EP, WIDE), bf16),
            pltpu.VMEM((80, WIDE), f32),
        ],
        compiler_params=pltpu.CompilerParams(vmem_limit_bytes=60 * 2**20),
    )(place, cameras, landmarks, packets, factors)


def eliminate_cameras(pair_cameras, cams, tiles, own_cameras):
    return pl.pallas_call(
        eliminate_cameras_kernel,
        out_shape=(jax.ShapeDtypeStruct((4, BW, 128), f32), jax.ShapeDtypeStruct((NB, BW, 128), f32)),
        in_specs=[SMEM, VMEM, VMEM, SMEM],
        out_specs=(VMEM, VMEM),
        scratch_shapes=[pltpu.VMEM((NB, BW, 128), f32)],
    )(pair_cameras, cams, tiles, own_cameras)


def local(jacobian, camera_block, landmark_block):
    place = (lax.axis_index("sub") % 8) * 2 + lax.axis_index("lm")
    blocks = jacobian[0]
    tiles = jnp.einsum("nrc,nrd->ncd", blocks, blocks, preferred_element_type=f32)
    cams = tiles[:, :BW, :BW].reshape(2, 2, BW, BW).transpose(0, 2, 1, 3).reshape(2, BW, 128)
    lower = tiles[:, BW:, :]
    numbers = jnp.concatenate([camera_block, landmark_block - NB], axis=0)
    ids = jnp.pad(numbers, ((0, 6), (0, 124)))
    dma = pltpu.SemaphoreType.DMA
    cams_all, ids_all = pl.pallas_call(
        trade_kernel,
        out_shape=(jax.ShapeDtypeStruct((4, 2, BW, 128), f32), jax.ShapeDtypeStruct((PEERS, 8, 128), jnp.int32)),
        in_specs=[VMEM, VMEM],
        out_specs=(VMEM, VMEM),
        scratch_shapes=[dma((4,)), dma((4,)), dma((PEERS,)), dma((PEERS,))],
        compiler_params=pltpu.CompilerParams(collective_id=0, has_side_effects=True),
    )(cams, ids)
    cameras = ids_all[:, 0, :4].reshape(64)
    landmarks = ids_all[:, 1, :4].reshape(64)
    pair_cameras = lax.dynamic_slice_in_dim(cameras, place // 4 * 16, 16)
    packets, factors = eliminate_cameras(pair_cameras, cams_all, lower, camera_block[0])
    packets_all = pl.pallas_call(
        gather_kernel,
        out_shape=jax.ShapeDtypeStruct((PEERS, 4, BW, 128), f32),
        in_specs=[VMEM],
        out_specs=VMEM,
        scratch_shapes=[dma((PEERS,)), dma((PEERS,)), dma((PEERS,))],
        compiler_params=pltpu.CompilerParams(collective_id=1, has_side_effects=True),
    )(packets)
    factor_rows, top = climb(place.reshape(1), cameras, landmarks, packets_all.reshape(64, BW, 128), factors)
    return factor_rows[:, None], top[:, None]


def solution(mesh):
    placed = (P("sub", "lm", None, None), P("sub", "lm"), P("sub", "lm"))
    return jax.shard_map(
        local,
        mesh=mesh,
        in_specs=placed,
        out_specs=(P(None, ("sub", "lm"), None, None), P(None, ("sub", "lm"), None, None)),
        check_vma=False,
    )
```

```python
import jax
import jax.numpy as jnp
from jax import lax
from jax.experimental import pallas as pl
from jax.experimental.pallas import tpu as pltpu
from jax.sharding import PartitionSpec as P

BW = 64
E = 576
NB = E // BW
EP = 640
WIDE = 3 * EP
PEERS = 16
MESH = pl.DeviceIdType.MESH
f32 = jnp.float32
bf16 = jnp.bfloat16


def lane_ids(shape):
    return lax.broadcasted_iota(jnp.int32, shape, 1)


def row_ids(shape):
    return lax.broadcasted_iota(jnp.int32, shape, 0)


def over_lanes(tile, column):
    return jnp.broadcast_to(tile[:, column : column + 1], tile.shape)


def over_rows(tile, row):
    return jnp.broadcast_to(tile[row : row + 1, :], tile.shape)


def factor_blocks(blocks):
    sub = row_ids((8, 128))
    mats = [[block[8 * i : 8 * i + 8, :] for i in range(8)] for block in blocks]
    for s in range(8):
        cols = [[[over_lanes(m[i], 8 * s + t) for i in range(s, 8)] for t in range(8)] for m in mats]
        pivots = [jnp.zeros((8, 128), f32) for _ in mats]
        for t in range(8):
            for b, m in enumerate(mats):
                row = over_rows(m[s], t)
                pivot = over_rows(cols[b][t][0], t)
                inverse = 1.0 / pivot
                pivots[b] = jnp.where(sub == t, pivot, pivots[b])
                scaled = [c * inverse for c in cols[b][t]]
                scaled[0] = jnp.where(sub > t, scaled[0], 0.0)
                for i in range(s, 8):
                    m[i] = m[i] - scaled[i - s] * row
                for u in range(t + 1, 8):
                    across = over_rows(cols[b][u][0], t)
                    for i in range(8 - s):
                        cols[b][u][i] = cols[b][u][i] - scaled[i] * across
        for b, m in enumerate(mats):
            m[s] = m[s] * lax.rsqrt(pivots[b])
    return [jnp.concatenate(m, axis=0) for m in mats]


def halves(value):
    high = value.astype(bf16)
    return high, (value - high.astype(f32)).astype(bf16)


def left_parts(value):
    high = value.astype(bf16).astype(f32)
    both = jnp.concatenate([high, value - high], axis=1).astype(bf16)
    return jnp.concatenate([both, high.astype(bf16)], axis=1)


def right_lanes(value):
    high = value.astype(bf16).astype(f32)
    both = jnp.concatenate([high, high], axis=1).astype(bf16)
    return jnp.concatenate([both, (value - high).astype(bf16)], axis=1)


def right_parts(value):
    high, low = halves(value)
    return jnp.concatenate([high, high, low], axis=0)


def mm(left, right):
    return jnp.dot(left, right, preferred_element_type=f32)


def mm_nt(left, right):
    return lax.dot_general(left, right, (((1,), (1,)), ((), ())), preferred_element_type=f32)


def group_place():
    return (lax.axis_index("sub") % 8) * 2 + lax.axis_index("lm")


def peer(mask):
    sub, lm = lax.axis_index("sub"), lax.axis_index("lm")
    step = mask // 2
    for bit in (1, 2, 4):
        if step & bit:
            sub = sub + bit - 2 * bit * ((sub // bit) % 2)
    if mask & 1:
        lm = 1 - lm
    return (sub, lm)


def relative(place, mask):
    for bit in (1, 2, 4, 8):
        if mask & bit:
            place = place + bit - 2 * bit * ((place // bit) % 2)
    return place


def greet(masks):
    barrier = pltpu.get_barrier_semaphore()
    for mask in masks:
        pl.semaphore_signal(barrier, inc=1, device_id=peer(mask), device_id_type=MESH)
    pl.semaphore_wait(barrier, len(masks))


ACROSS = (1, 5, 8, 9, 13, 4, 12)
FIRST, SECOND = slice(0, 2), slice(2, 4)
WHOLE = slice(0, 4)
PIECES = {
    "near": (1, WHOLE), "wrap": (5, WHOLE), "row": (8, WHOLE), "far_a": (4, FIRST), "far_b": (4, SECOND),
    "row_near": (9, WHOLE), "row_wrap": (13, WHOLE), "row_far_a": (12, FIRST), "row_far_b": (12, SECOND),
}
NAMES = tuple(PIECES)


def exchange_kernel(
    cam_ref, lmk_ref, tiles_ref, raw_ref, fac_ref, last_ref, ids_ref,
    cams_own, cams, fac_own, last_own,
    cam_send, cam_recv, id_send, id_recv, raw_send, raw_recv, pass_send, pass_recv,
    fac_send, fac_recv, fac_pass, last_send, last_recv,
):
    place = group_place()
    greet(range(1, PEERS))
    lane = lane_ids((BW, 128))
    row = row_ids((BW, 128))

    def remote(src, dst, send, recv, mask):
        return pltpu.make_async_remote_copy(src, dst, send, recv, device_id=peer(mask), device_id_type=MESH)

    for b in range(2):
        cams_own[b] = jnp.where(
            lane < BW, tiles_ref[2 * b, 0:BW, :], pltpu.roll(tiles_ref[2 * b + 1, 0:BW, :], BW, 1)
        )
    for b in range(4):
        ids_ref[pl.ds(place, 1), b:b + 1, :] = jnp.full((1, 1, 128), cam_ref[0, b], jnp.int32)
        ids_ref[pl.ds(place, 1), 4 + b:5 + b, :] = jnp.full((1, 1, 128), lmk_ref[0, b], jnp.int32)
    quick = [remote(cams_own, cams.at[place % 4], cam_send.at[mask], cam_recv.at[mask], mask) for mask in (3, 1, 2)]
    numbers = {
        mask: remote(ids_ref.at[place], ids_ref.at[place], id_send.at[mask], id_recv.at[mask], mask)
        for mask in (3, 1, 2) + tuple(range(4, PEERS))
    }
    for copy in quick:
        copy.start()
    for copy in numbers.values():
        copy.start()
    started = quick + list(numbers.values())

    own_tiles = tiles_ref.at[:, BW:2 * BW, :]
    arrivals = {}

    def piece(name, source, mask):
        at = NAMES.index(name)
        owner, part = PIECES[name]
        source_place = relative(relative(place, mask), owner)
        copy = remote(source, raw_ref.at[source_place, part], raw_send.at[at], raw_recv.at[at], mask)
        copy.start()
        arrivals[name] = copy

    piece("near", own_tiles, 1)
    piece("wrap", own_tiles, 5)
    piece("row", own_tiles, 8)
    to_core = []

    def share(at, source, slot):
        copy = remote(source, slot, pass_send.at[at], pass_recv.at[at], 2)
        copy.start()
        to_core.append(copy)

    def landed(name):
        arrivals[name].wait_recv()
        owner, part = PIECES[name]
        slot = raw_ref.at[relative(place, owner), part]
        share(NAMES.index(name), slot, slot)
        return slot

    share(len(NAMES), own_tiles, raw_ref.at[place])
    raw_ref[pl.ds(place, 1)] = tiles_ref[:, BW:2 * BW, :][None]
    cams[pl.ds(place % 4, 1)] = cams_own[...][None]

    for copy in quick:
        copy.wait_recv()
    for mask in (3, 1, 2):
        numbers[mask].wait_recv()
    quarter = place % 4
    start = jnp.where(lane == row, 2.0, jnp.where(lane == row + BW, 1.0, 0.0)).astype(f32)
    totals = [start, start, start]
    wanted = (quarter, quarter + 4, 8)
    for d in range(4):
        device = place - quarter + d
        for b in range(4):
            packed = cams[d, b // 2]
            if b % 2:
                packed = pltpu.roll(packed, BW, 1)
            packed = jnp.where(lane < BW, packed, 0.0)
            number = ids_ref[pl.ds(device, 1), b:b + 1, :].reshape(1, 128)
            for u in range(3):
                totals[u] = totals[u] + jnp.where(number == wanted[u], packed, 0.0)

    for name, mask in (("near", 5), ("wrap", 1), ("row", 1)):
        slot = landed(name)
        if name == "near":
            piece("far_a", slot.at[FIRST], 5)
        elif name == "wrap":
            piece("far_b", slot.at[SECOND], 1)
        else:
            piece("row_near", slot, 1)
            piece("row_wrap", slot, 5)

    mixed = []
    for block in factor_blocks(totals):
        mixed.append(jnp.where(lane >= row, block, pltpu.roll(block, BW, 1)))
    fac_own[...] = jnp.where(lane < BW, mixed[0], pltpu.roll(mixed[1], BW, 1))
    half = BW // 2
    last = jnp.concatenate([mixed[2][:half, :BW], mixed[2][half:, :BW]], axis=1)
    last_own[...] = last
    facs = {}
    for mask in ACROSS + (2,):
        facs[mask] = remote(fac_own, fac_ref.at[place], fac_send.at[mask], fac_recv.at[mask], mask)
        facs[mask].start()
    lasts = []
    for n, mask in enumerate((4, 8, 12)):
        copy = remote(last_own, last_ref.at[place // 4], last_send.at[n], last_recv.at[n], mask)
        copy.start()
        lasts.append(copy)
    fac_ref[pl.ds(place, 1)] = fac_own[...][None]
    last_ref[pl.ds(place // 4, 1)] = last[None]

    piece("row_far_a", landed("far_a"), 8)
    piece("row_far_b", landed("far_b"), 8)
    landed("row_near")
    landed("row_wrap")
    passed = []
    for mask in ACROSS:
        facs[mask].wait_recv()
        slot = fac_ref.at[relative(place, mask)]
        copy = remote(slot, slot, fac_pass.at[mask], fac_recv.at[mask ^ 2], 2)
        copy.start()
        passed.append(copy)
    landed("row_far_a")
    landed("row_far_b")
    facs[2].wait_recv()
    for copy in passed + lasts + to_core:
        copy.wait()
    for mask in range(4, PEERS):
        numbers[mask].wait_recv()
    for copy in started + list(facs.values()) + list(arrivals.values()):
        copy.wait_send()


def eliminate(fronts, own=None):
    lane = lane_ids((BW, 128))
    row = row_ids((BW, 128))
    unit = jnp.where(lane == row + BW, 1.0, 0.0).astype(f32)
    diag = [front[0:BW, 0:128] for front in fronts]
    for k in range(NB):
        r0, t0 = BW * k, k // 2 * 128
        r1, t1 = r0 + BW, (k + 1) // 2 * 128
        if k % 2:
            diag = [pltpu.roll(tile, BW, 1) for tile in diag]
        done = factor_blocks([jnp.where(lane < BW, tile, unit) for tile in diag])
        following = []
        for front, block in zip(fronts, done):
            inverse = pltpu.roll(block, BW, 1)[:, :BW]
            upper = mm(left_parts(inverse), right_parts(front[r0:r1, t0:WIDE]))
            corner = jnp.where(jnp.logical_and(lane >= row, lane < BW), block, 0.0)
            if k % 2:
                first = pltpu.roll(corner, BW, 1)
            else:
                first = jnp.where(lane < BW, corner, upper[:, :128])
            front[r0:r1, t0:t0 + 128] = first
            front[r0:r1, t0 + 128:WIDE] = upper[:, 128:]
            high, low = halves(upper)
            parts = jnp.concatenate([high, high, low], axis=0)
            left = None
            if k < NB - 1:
                turned = upper[:, t1 - t0:EP - t0].T
                left = left_parts(turned[r1 - t1:E - t1])
                following.append(front[r1:r1 + BW, t1:t1 + 128] - mm(left[:BW], parts[:, t1 - t0:t1 - t0 + 128]))
            if own is not None:
                block_lanes = own[:, r0:r1]
                own_solved = mm_nt(left_parts(block_lanes), right_lanes(inverse))
                own_left = left_parts(own_solved)
            begin = t1 if k < NB - 1 else EP
            bounds = [n for n in (0, 256, 512, 640, 896, 1152, 1408, 1664, 1920) if n > begin]
            for n1 in bounds:
                n0 = begin
                begin = n1
                last = min(E, n1)
                piece = parts[:, n0 - t0:n1 - t0]
                if left is not None:
                    front[r1:last, n0:n1] = front[r1:last, n0:n1] - mm(left[:last - r1], piece)
                if own is not None:
                    own[:, n0:n1] = own[:, n0:n1] - mm(own_left, piece)
            if own is not None:
                own[:, r0:r1] = own_solved
        diag = following


def climb_kernel(
    ids_ref, raw_ref, fac_ref, last_ref, out_ref, top_ref,
    front, upper_front, private, spread, spread_high, spread_low, rows21, rows11, left_all, own, packet_ref, solver, stage,
):
    place = group_place()
    lane = lane_ids((BW, 128))
    row = row_ids((BW, 128))
    zero_tile = jnp.zeros((BW, 128), f32)

    def clear(ref, count, width):
        def step(i, carry):
            ref[pl.ds(pl.multiple_of(i * BW, BW), BW), :] = jnp.zeros((BW, width), f32)
            return carry

        lax.fori_loop(0, count // BW, step, 0)

    for g in range(2):
        clear(front.at[g], EP, WIDE)
    for m in range(4):
        for n in range(5):
            clear(private.at[m, n], EP, 128)
    clear(upper_front, EP, WIDE)
    for n in range(5):
        clear(rows21.at[0, n], 2 * EP, 128)
        clear(rows11.at[n], EP, 128)
    own[...] = jnp.zeros(own.shape, f32)
    for i in range(NB):
        spot = jnp.where(lane == row + BW * (i % 2), 1.0, 0.0).astype(f32)
        tile = (slice(BW * i, BW * i + BW), slice(i // 2 * 128, i // 2 * 128 + 128))
        for g in range(2):
            front[(g,) + tile] = 2.0 * spot
        for m in range(4):
            private[m, i // 2, BW * i:BW * i + BW, :] = spot

    def numbers(j):
        return ids_ref[j // 4, j % 4, 0], ids_ref[j // 4, 4 + j % 4, 0] - NB

    pair = place // 4

    def camera_factor(p, c):
        if c < 8:
            both = fac_ref[4 * p + c % 4]
            return pltpu.roll(both, BW, 1) if c >= 4 else both
        both = last_ref[p]
        return jnp.concatenate([both, pltpu.roll(both, BW, 1)], axis=0)

    for p in range(4):
        for c in range(NB):
            mixed = camera_factor(p, c)
            inverse = jnp.where(lane < row, mixed, jnp.where(lane == row, 1.0 / mixed, 0.0))
            solver[NB * p + c] = right_lanes(inverse[:, :BW])
    for p in range(4):
        for b in range(16):
            j = 16 * p + b
            c, _ = numbers(j)
            raw = raw_ref[4 * p + b // 4, b % 4]
            solved = mm_nt(left_parts(raw[:, :BW]), solver[NB * p + c])
            packet_ref[j] = jnp.where(lane < BW, jnp.concatenate([solved, solved], axis=1), raw)

    for b in range(16):
        j = pair * 16 + b
        c, l = numbers(j)
        packet = packet_ref[j]
        side = c % 2
        both = jnp.where(lane < BW, packet, pltpu.roll(packet, BW, 1))
        placed = jnp.where(lane // BW == side, both, 0.0)
        spot = (0, c // 2, pl.ds(pl.multiple_of(b // 8 * EP + l * BW, BW), BW), slice(None))
        rows21[spot] = rows21[spot] + placed
    for c in range(NB):
        turned = camera_factor(pair, c).T[:BW]
        keep = lane_ids((BW, BW)) <= row_ids((BW, BW))
        rows11[c // 2, BW * c:BW * c + BW, c % 2 * BW:c % 2 * BW + BW] = jnp.where(keep, turned, 0.0)
    place0 = place % 4
    for n in range(0, EP, 128):
        stage[0, 0:144, n:n + 128] = rows11[n // 128, pl.ds(place0, 144, stride=4), :]
        stage[1, 0:144, n:n + 128] = rows21[0, n // 128, pl.ds(place0, 144, stride=4), :]
        stage[2, 0:144, n:n + 128] = rows21[0, n // 128, pl.ds(EP + place0, 144, stride=4), :]

    for m in range(4):
        g, h = m // 2, m % 2

        def clear_spread(c, carry):
            spread[c] = jnp.zeros((BW, 2 * EP), f32)
            return carry

        lax.fori_loop(0, NB, clear_spread, 0)
        for b in range(16):
            j = 16 * m + b
            c, l = numbers(j)
            packet = packet_ref[j]
            side = l % 2
            across = packet.T[:BW]
            both = jnp.concatenate([across, across], axis=1)
            placed = jnp.where(lane // BW == side, both, 0.0)
            spot = (c, slice(None), pl.ds(pl.multiple_of(b // 8 * EP + l // 2 * 128, 128), 128))
            spread[spot] = spread[spot] + placed
            squares = jnp.where(lane >= BW, packet, pltpu.roll(packet, BW, 1))
            squares = jnp.where(lane // BW == side, squares, 0.0)
            rows = pl.ds(pl.multiple_of(l * BW, BW), BW)
            if b < 8:
                spot = (g, rows, pl.ds(pl.multiple_of(l // 2 * 128, 128), 128))
                front[spot] = front[spot] + squares
            else:
                spot = (m, l // 2, rows, slice(None))
                private[spot] = private[spot] + squares

        def split_spread(c, carry):
            high, low = halves(spread[c])
            spread_high[c] = high
            spread_low[c] = low
            return carry

        lax.fori_loop(0, NB, split_spread, 0)
        for b in range(16):
            j = 16 * m + b
            c, l = numbers(j)
            left = left_parts(packet_ref[j][:, :BW])
            rows = pl.ds(pl.multiple_of(l * BW, BW), BW)
            begin = 0 if b < 8 else EP
            high = spread_high[c, :, begin:]
            taken = mm(left, jnp.concatenate([high, high, spread_low[c, :, begin:]], axis=0))
            if b < 8:
                front[g, rows, 0:EP] = front[g, rows, 0:EP] - taken[:, :EP]
                front[g, rows, EP * (1 + h):EP * (2 + h)] = front[g, rows, EP * (1 + h):EP * (2 + h)] - taken[:, EP:]
            else:
                for n in range(5):
                    private[m, n, rows, :] = private[m, n, rows, :] - taken[:, 128 * n:128 * n + 128]

    eliminate([front.at[0], front.at[1]])
    place1 = place % 8
    mine = place // 8
    for g in range(2):
        for j in range(5):
            for i in range(10):
                rows21[g, j, 128 * i:128 * i + 128, :] = front[
                    g, 128 * j:128 * j + 128, EP + 128 * i:EP + 128 * i + 128
                ].T
    for j in range(5):
        for i in range(j, 5):
            rows11[j, 128 * i:128 * i + 128, :] = front[
                mine, 128 * j:128 * j + 128, 128 * i:128 * i + 128
            ].T
        for i in range(j):
            rows11[j, 128 * i:128 * i + 128, :] = jnp.zeros((128, 128), f32)
    for n in range(0, EP, 128):
        stage[0, 144:216, n:n + 128] = rows11[n // 128, pl.ds(place1, 72, stride=8), :]
        stage[1, 144:216, n:n + 128] = rows21[mine, n // 128, pl.ds(place1, 72, stride=8), :]
        stage[2, 144:216, n:n + 128] = rows21[mine, n // 128, pl.ds(EP + place1, 72, stride=8), :]
    for g in range(2):
        for n in range(0, EP, 128):
            high, low = halves(rows21[g, n // 128, 0:E, :])
            left_all[g, 0:E, n:n + 128] = high
            left_all[g, 0:E, EP + n:EP + n + 128] = low
            left_all[g, 0:E, 2 * EP + n:2 * EP + n + 128] = high
            few = rows21[g, n // 128, pl.ds(EP + place, 40, stride=16), :]
            high, low = halves(jnp.concatenate([few, jnp.zeros((24, 128), f32)], axis=0))
            left_all[g, E:EP, n:n + 128] = high
            left_all[g, E:EP, EP + n:EP + n + 128] = low
            left_all[g, E:EP, 2 * EP + n:2 * EP + n + 128] = high
        for n0, n1 in ((0, 256), (256, 512), (512, 640), (640, 896), (896, 1152), (1152, 1280)):
            high, low = halves(front[g, :, EP + n0:EP + n1])
            taken = mm(left_all[g], jnp.concatenate([high, high, low], axis=0))
            if n0 < EP:
                base = jnp.concatenate([private[2 * g, n // 128, 0:E, :] for n in range(n0, n1, 128)], axis=1) - taken[:E]
                if g:
                    base = base + upper_front[0:E, n0:n1]
                upper_front[0:E, n0:n1] = base
                own[40 * g:40 * g + 40, n0:n1] = -taken[E:E + 40]
            else:
                shift = EP * g
                upper_front[0:E, n0 + shift:n1 + shift] = -taken[:E]
                for n in range(n0, n1, 128):
                    kept = private[2 * g + 1, (n - EP) // 128, pl.ds(place, 40, stride=16), :]
                    own[40 * g:40 * g + 40, n + shift:n + shift + 128] = kept - taken[E:E + 40, n - n0:n - n0 + 128]

    eliminate([upper_front], own)
    for j in range(5):
        for i in range(j, 5):
            rows11[j, 128 * i:128 * i + 128, :] = upper_front[
                128 * j:128 * j + 128, 128 * i:128 * i + 128
            ].T
    for n in range(0, EP, 128):
        stage[0, 216:252, n:n + 128] = rows11[n // 128, pl.ds(place, 36, stride=16), :]
    for h in range(2):
        stage[1 + h, 216:252, :] = own[40 * h:40 * h + 36, 0:EP]
        top_ref[h, :, 0:E] = own[40 * h:40 * h + 36, EP:EP + E]
        top_ref[h, :, E:2 * E] = own[40 * h:40 * h + 36, 2 * EP:2 * EP + E]
    for h in range(3):
        for n in range(0, E, 128):
            tall = min(128, E - n)
            for r in range(0, 256, 128):
                wide = min(128, 252 - r)
                out_ref[h, n:n + tall, r:r + wide] = stage[h, r:r + 128, n:n + 128].T[:tall, :wide]


VMEM = pl.BlockSpec(memory_space=pltpu.VMEM)
SMEM = pl.BlockSpec(memory_space=pltpu.SMEM)


def climb(ids, raw, factors, last):
    return pl.pallas_call(
        climb_kernel,
        out_shape=(jax.ShapeDtypeStruct((3, E, 252), f32), jax.ShapeDtypeStruct((2, 36, 2 * E), f32)),
        in_specs=[SMEM, VMEM, VMEM, VMEM],
        out_specs=(VMEM, VMEM),
        scratch_shapes=[
            pltpu.VMEM((2, EP, WIDE), f32),
            pltpu.VMEM((EP, WIDE), f32),
            pltpu.VMEM((4, 5, EP, 128), f32),
            pltpu.VMEM((NB, BW, 2 * EP), f32),
            pltpu.VMEM((NB, BW, 2 * EP), bf16),
            pltpu.VMEM((NB, BW, 2 * EP), bf16),
            pltpu.VMEM((2, 5, 2 * EP, 128), f32),
            pltpu.VMEM((5, EP, 128), f32),
            pltpu.VMEM((2, EP, WIDE), bf16),
            pltpu.VMEM((80, WIDE), f32),
            pltpu.VMEM((64, BW, 128), f32),
            pltpu.VMEM((4 * NB, BW, 3 * BW), bf16),
            pltpu.VMEM((3, 256, EP), f32),
        ],
        compiler_params=pltpu.CompilerParams(vmem_limit_bytes=60 * 2**20),
    )(ids, raw, factors, last)


def exchange(cameras, landmarks, tiles):
    dma = pltpu.SemaphoreType.DMA
    return pl.pallas_call(
        exchange_kernel,
        out_shape=(
            jax.ShapeDtypeStruct((PEERS, 4, BW, 128), f32),
            jax.ShapeDtypeStruct((PEERS, BW, 128), f32),
            jax.ShapeDtypeStruct((4, BW // 2, 128), f32),
            jax.ShapeDtypeStruct((PEERS, 8, 128), jnp.int32),
        ),
        in_specs=[SMEM, SMEM, VMEM],
        out_specs=(VMEM, VMEM, VMEM, VMEM),
        scratch_shapes=[
            pltpu.VMEM((2, BW, 128), f32),
            pltpu.VMEM((4, 2, BW, 128), f32),
            pltpu.VMEM((BW, 128), f32),
            pltpu.VMEM((BW // 2, 128), f32),
            dma((4,)), dma((4,)), dma((PEERS,)), dma((PEERS,)),
            dma((9,)), dma((9,)), dma((10,)), dma((10,)),
            dma((PEERS,)), dma((PEERS,)), dma((PEERS,)), dma((3,)), dma((3,)),
        ],
        compiler_params=pltpu.CompilerParams(collective_id=0, has_side_effects=True),
    )(cameras, landmarks, tiles)


def local(jacobian, camera_block, landmark_block):
    blocks = jacobian[0]
    tiles = jnp.einsum("nrc,nrd->ncd", blocks, blocks, preferred_element_type=f32)
    raw, factors, last, ids = exchange(camera_block, landmark_block, tiles)
    factor_rows, top = climb(ids, raw, factors, last)
    return factor_rows.transpose(0, 2, 1)[:, None], top[:, None]


def solution(mesh):
    placed = (P("sub", "lm", None, None), P("sub", "lm"), P("sub", "lm"))
    return jax.shard_map(
        local,
        mesh=mesh,
        in_specs=placed,
        out_specs=(P(None, ("sub", "lm"), None, None), P(None, ("sub", "lm"), None, None)),
        check_vma=False,
    )
```

```python
import jax
import jax.numpy as jnp
from jax import lax
from jax.experimental import pallas as pl
from jax.experimental.pallas import tpu as pltpu
from jax.sharding import PartitionSpec as P

BW = 64
E = 576
NB = E // BW
EP = 640
WIDE = 3 * EP
PEERS = 16
MESH = pl.DeviceIdType.MESH
f32 = jnp.float32
bf16 = jnp.bfloat16


def lane_ids(shape):
    return lax.broadcasted_iota(jnp.int32, shape, 1)


def row_ids(shape):
    return lax.broadcasted_iota(jnp.int32, shape, 0)


def over_lanes(tile, column):
    return jnp.broadcast_to(tile[:, column : column + 1], tile.shape)


def over_rows(tile, row):
    return jnp.broadcast_to(tile[row : row + 1, :], tile.shape)


def factor_blocks(blocks):
    sub = row_ids((8, 128))
    mats = [[block[8 * i : 8 * i + 8, :] for i in range(8)] for block in blocks]
    for s in range(8):
        cols = [[[over_lanes(m[i], 8 * s + t) for i in range(s, 8)] for t in range(8)] for m in mats]
        pivots = [jnp.zeros((8, 128), f32) for _ in mats]
        for t in range(8):
            for b, m in enumerate(mats):
                row = over_rows(m[s], t)
                pivot = over_rows(cols[b][t][0], t)
                inverse = 1.0 / pivot
                pivots[b] = jnp.where(sub == t, pivot, pivots[b])
                scaled = [c * inverse for c in cols[b][t]]
                scaled[0] = jnp.where(sub > t, scaled[0], 0.0)
                for i in range(s, 8):
                    m[i] = m[i] - scaled[i - s] * row
                for u in range(t + 1, 8):
                    across = over_rows(cols[b][u][0], t)
                    for i in range(8 - s):
                        cols[b][u][i] = cols[b][u][i] - scaled[i] * across
        for b, m in enumerate(mats):
            m[s] = m[s] * lax.rsqrt(pivots[b])
    return [jnp.concatenate(m, axis=0) for m in mats]


def halves(value):
    high = value.astype(bf16)
    return high, (value - high.astype(f32)).astype(bf16)


def left_parts(value):
    high = value.astype(bf16).astype(f32)
    both = jnp.concatenate([high, value - high], axis=1).astype(bf16)
    return jnp.concatenate([both, high.astype(bf16)], axis=1)


def right_lanes(value):
    high = value.astype(bf16).astype(f32)
    both = jnp.concatenate([high, high], axis=1).astype(bf16)
    return jnp.concatenate([both, (value - high).astype(bf16)], axis=1)


def right_parts(value):
    high, low = halves(value)
    return jnp.concatenate([high, high, low], axis=0)


def mm(left, right):
    return jnp.dot(left, right, preferred_element_type=f32)


def mm_nt(left, right):
    return lax.dot_general(left, right, (((1,), (1,)), ((), ())), preferred_element_type=f32)


def group_place():
    return (lax.axis_index("sub") % 8) * 2 + lax.axis_index("lm")


def peer(mask):
    sub, lm = lax.axis_index("sub"), lax.axis_index("lm")
    step = mask // 2
    for bit in (1, 2, 4):
        if step & bit:
            sub = sub + bit - 2 * bit * ((sub // bit) % 2)
    if mask & 1:
        lm = 1 - lm
    return (sub, lm)


def relative(place, mask):
    for bit in (1, 2, 4, 8):
        if mask & bit:
            place = place + bit - 2 * bit * ((place // bit) % 2)
    return place


def greet(masks):
    barrier = pltpu.get_barrier_semaphore()
    for mask in masks:
        pl.semaphore_signal(barrier, inc=1, device_id=peer(mask), device_id_type=MESH)
    pl.semaphore_wait(barrier, len(masks))


ACROSS = (1, 5, 8, 9, 13, 4, 12)
FIRST, SECOND = slice(0, 2), slice(2, 4)
WHOLE = slice(0, 4)
PIECES = {
    "near": (1, WHOLE), "wrap": (5, WHOLE), "row": (8, WHOLE), "far_a": (4, FIRST), "far_b": (4, SECOND),
    "row_near": (9, WHOLE), "row_wrap": (13, WHOLE), "row_far_a": (12, FIRST), "row_far_b": (12, SECOND),
}
NAMES = tuple(PIECES)


def exchange_kernel(
    cam_ref, lmk_ref, tiles_ref, raw_ref, fac_ref, last_ref, ids_ref,
    cams_own, cams, fac_own, last_own,
    cam_send, cam_recv, id_send, id_recv, raw_send, raw_recv, pass_send, pass_recv,
    fac_send, fac_recv, fac_pass, last_send, last_recv,
):
    place = group_place()
    greet(range(1, PEERS))
    lane = lane_ids((BW, 128))
    row = row_ids((BW, 128))

    def remote(src, dst, send, recv, mask):
        return pltpu.make_async_remote_copy(src, dst, send, recv, device_id=peer(mask), device_id_type=MESH)

    for b in range(2):
        cams_own[b] = jnp.where(
            lane < BW, tiles_ref[2 * b, 0:BW, :], pltpu.roll(tiles_ref[2 * b + 1, 0:BW, :], BW, 1)
        )
    for b in range(4):
        ids_ref[pl.ds(place, 1), b:b + 1, :] = jnp.full((1, 1, 128), cam_ref[0, b], jnp.int32)
        ids_ref[pl.ds(place, 1), 4 + b:5 + b, :] = jnp.full((1, 1, 128), lmk_ref[0, b], jnp.int32)
    quick = [remote(cams_own, cams.at[place % 4], cam_send.at[mask], cam_recv.at[mask], mask) for mask in (3, 1, 2)]
    numbers = {
        mask: remote(ids_ref.at[place], ids_ref.at[place], id_send.at[mask], id_recv.at[mask], mask)
        for mask in (3, 1, 2) + tuple(range(4, PEERS))
    }
    for copy in quick:
        copy.start()
    for copy in numbers.values():
        copy.start()
    started = quick + list(numbers.values())

    own_tiles = tiles_ref.at[:, BW:2 * BW, :]
    arrivals = {}

    def piece(name, source, mask):
        at = NAMES.index(name)
        owner, part = PIECES[name]
        source_place = relative(relative(place, mask), owner)
        copy = remote(source, raw_ref.at[source_place, part], raw_send.at[at], raw_recv.at[at], mask)
        copy.start()
        arrivals[name] = copy

    piece("near", own_tiles, 1)
    piece("wrap", own_tiles, 5)
    piece("row", own_tiles, 8)
    to_core = []

    def share(at, source, slot):
        copy = remote(source, slot, pass_send.at[at], pass_recv.at[at], 2)
        copy.start()
        to_core.append(copy)

    def landed(name):
        arrivals[name].wait_recv()
        owner, part = PIECES[name]
        slot = raw_ref.at[relative(place, owner), part]
        share(NAMES.index(name), slot, slot)
        return slot

    share(len(NAMES), own_tiles, raw_ref.at[place])
    raw_ref[pl.ds(place, 1)] = tiles_ref[:, BW:2 * BW, :][None]
    cams[pl.ds(place % 4, 1)] = cams_own[...][None]

    for copy in quick:
        copy.wait_recv()
    for mask in (3, 1, 2):
        numbers[mask].wait_recv()
    quarter = place % 4
    start = jnp.where(lane == row, 2.0, jnp.where(lane == row + BW, 1.0, 0.0)).astype(f32)
    totals = [start, start, start]
    wanted = (quarter, quarter + 4, 8)
    for d in range(4):
        device = place - quarter + d
        for b in range(4):
            packed = cams[d, b // 2]
            if b % 2:
                packed = pltpu.roll(packed, BW, 1)
            packed = jnp.where(lane < BW, packed, 0.0)
            number = ids_ref[pl.ds(device, 1), b:b + 1, :].reshape(1, 128)
            for u in range(3):
                totals[u] = totals[u] + jnp.where(number == wanted[u], packed, 0.0)

    for name, mask in (("near", 5), ("wrap", 1), ("row", 1)):
        slot = landed(name)
        if name == "near":
            piece("far_a", slot.at[FIRST], 5)
        elif name == "wrap":
            piece("far_b", slot.at[SECOND], 1)
        else:
            piece("row_near", slot, 1)
            piece("row_wrap", slot, 5)

    mixed = []
    for block in factor_blocks(totals):
        mixed.append(jnp.where(lane >= row, block, pltpu.roll(block, BW, 1)))
    fac_own[...] = jnp.where(lane < BW, mixed[0], pltpu.roll(mixed[1], BW, 1))
    half = BW // 2
    last = jnp.concatenate([mixed[2][:half, :BW], mixed[2][half:, :BW]], axis=1)
    last_own[...] = last
    facs = {}
    for mask in ACROSS + (2,):
        facs[mask] = remote(fac_own, fac_ref.at[place], fac_send.at[mask], fac_recv.at[mask], mask)
        facs[mask].start()
    lasts = []
    for n, mask in enumerate((4, 8, 12)):
        copy = remote(last_own, last_ref.at[place // 4], last_send.at[n], last_recv.at[n], mask)
        copy.start()
        lasts.append(copy)
    fac_ref[pl.ds(place, 1)] = fac_own[...][None]
    last_ref[pl.ds(place // 4, 1)] = last[None]

    piece("row_far_a", landed("far_a"), 8)
    piece("row_far_b", landed("far_b"), 8)
    landed("row_near")
    landed("row_wrap")
    passed = []
    for mask in ACROSS:
        facs[mask].wait_recv()
        slot = fac_ref.at[relative(place, mask)]
        copy = remote(slot, slot, fac_pass.at[mask], fac_recv.at[mask ^ 2], 2)
        copy.start()
        passed.append(copy)
    landed("row_far_a")
    landed("row_far_b")
    facs[2].wait_recv()
    for copy in passed + lasts + to_core:
        copy.wait()
    for mask in range(4, PEERS):
        numbers[mask].wait_recv()
    for copy in started + list(facs.values()) + list(arrivals.values()):
        copy.wait_send()


def eliminate(fronts, own=None):
    lane = lane_ids((BW, 128))
    row = row_ids((BW, 128))
    unit = jnp.where(lane == row + BW, 1.0, 0.0).astype(f32)
    diag = [front[0:BW, 0:128] for front in fronts]
    for k in range(NB):
        r0, t0 = BW * k, k // 2 * 128
        r1, t1 = r0 + BW, (k + 1) // 2 * 128
        if k % 2:
            diag = [pltpu.roll(tile, BW, 1) for tile in diag]
        done = factor_blocks([jnp.where(lane < BW, tile, unit) for tile in diag])
        following = []
        for front, block in zip(fronts, done):
            inverse = pltpu.roll(block, BW, 1)[:, :BW]
            upper = mm(left_parts(inverse), right_parts(front[r0:r1, t0:WIDE]))
            corner = jnp.where(jnp.logical_and(lane >= row, lane < BW), block, 0.0)
            if k % 2:
                first = pltpu.roll(corner, BW, 1)
            else:
                first = jnp.where(lane < BW, corner, upper[:, :128])
            front[r0:r1, t0:t0 + 128] = first
            front[r0:r1, t0 + 128:WIDE] = upper[:, 128:]
            high, low = halves(upper)
            parts = jnp.concatenate([high, high, low], axis=0)
            left = None
            if k < NB - 1:
                turned = upper[:, t1 - t0:EP - t0].T
                left = left_parts(turned[r1 - t1:E - t1])
                following.append(front[r1:r1 + BW, t1:t1 + 128] - mm(left[:BW], parts[:, t1 - t0:t1 - t0 + 128]))
            if own is not None:
                block_lanes = own[:, r0:r1]
                own_solved = mm_nt(left_parts(block_lanes), right_lanes(inverse))
                own_left = left_parts(own_solved)
            begin = t1 if k < NB - 1 else EP
            bounds = [n for n in (0, 256, 512, 640, 896, 1152, 1408, 1664, 1920) if n > begin]
            for n1 in bounds:
                n0 = begin
                begin = n1
                last = min(E, n1)
                piece = parts[:, n0 - t0:n1 - t0]
                if left is not None:
                    front[r1:last, n0:n1] = front[r1:last, n0:n1] - mm(left[:last - r1], piece)
                if own is not None:
                    own[:, n0:n1] = own[:, n0:n1] - mm(own_left, piece)
            if own is not None:
                own[:, r0:r1] = own_solved
        diag = following


def groups_kernel(
    ids_ref, raw_ref, fac_ref, last_ref, early_ref, rows_ref, front_out, own_out,
    front, private, spread, spread_high, spread_low, rows21, rows11, left_all, packet_ref, solver,
):
    place = group_place()
    core = place // 2 % 2
    sibling = place + 2 - 4 * core
    pair = place // 4
    lane = lane_ids((BW, 128))
    row = row_ids((BW, 128))

    def clear(ref, first, count, width):
        def step(i, carry):
            ref[pl.ds(pl.multiple_of(first + i * BW, BW), BW), :] = jnp.zeros((BW, width), f32)
            return carry

        lax.fori_loop(0, count // BW, step, 0)

    clear(front, 0, EP, WIDE)
    for m in range(2):
        for n in range(5):
            clear(private.at[m, n], 0, EP, 128)
    for h in range(3):
        early_ref[h] = jnp.zeros((144, EP), f32)
    for i in range(NB):
        spot = jnp.where(lane == row + BW * (i % 2), 1.0, 0.0).astype(f32)
        front[BW * i:BW * i + BW, i // 2 * 128:i // 2 * 128 + 128] = 2.0 * spot
        for m in range(2):
            private[m, i // 2, BW * i:BW * i + BW, :] = spot

    def numbers(j):
        return ids_ref[j // 4, j % 4, 0], ids_ref[j // 4, 4 + j % 4, 0] - NB

    def camera_factor(p, c):
        if c < 8:
            both = fac_ref[4 * p + c % 4]
            return pltpu.roll(both, BW, 1) if c >= 4 else both
        both = last_ref[p]
        return jnp.concatenate([both, pltpu.roll(both, BW, 1)], axis=0)

    for u, p in enumerate((2 * core, 2 * core + 1, pair)):
        for c in range(NB):
            mixed = camera_factor(p, c)
            inverse = jnp.where(lane < row, mixed, jnp.where(lane == row, 1.0 / mixed, 0.0))
            solver[NB * u + c] = right_lanes(inverse[:, :BW])
    for j in range(32):
        c, _ = numbers(32 * core + j)
        raw = raw_ref[8 * core + j // 4, j % 4]
        solved = mm_nt(left_parts(raw[:, :BW]), solver[NB * (j // 16) + c])
        packet_ref[j] = jnp.where(lane < BW, jnp.concatenate([solved, solved], axis=1), raw)

    quarter = place % 4
    few = lane_ids((16, 128))
    for b in range(16):
        c, l = numbers(pair * 16 + b)
        raw = raw_ref[4 * pair + b // 4, b % 4, pl.ds(quarter, 16, stride=4), :]
        solved = mm_nt(left_parts(raw[:, :BW]), solver[2 * NB + c])
        placed = jnp.where(few // BW == c % 2, jnp.concatenate([solved, solved], axis=1), 0.0)
        spot = (1 + b // 8, pl.ds(pl.multiple_of(l * 16, 16), 16), pl.ds(pl.multiple_of(c // 2 * 128, 128), 128))
        early_ref[spot] = early_ref[spot] + placed
    for c in range(NB):
        turned = camera_factor(pair, c).T[:BW]
        keep = lane_ids((BW, BW)) <= row_ids((BW, BW))
        rows11[c // 2, BW * c:BW * c + BW, c % 2 * BW:c % 2 * BW + BW] = jnp.where(keep, turned, 0.0)
    for c in range(NB):
        few_rows = rows11[c // 2, pl.ds(BW * c + quarter, 16, stride=4), :]
        early_ref[0, 16 * c:16 * c + 16, c // 2 * 128:c // 2 * 128 + 128] = jnp.where(few // BW == c % 2, few_rows, 0.0)

    for m in range(2):

        def clear_spread(c, carry):
            spread[c] = jnp.zeros((BW, 2 * EP), f32)
            return carry

        lax.fori_loop(0, NB, clear_spread, 0)
        for b in range(16):
            c, l = numbers(32 * core + 16 * m + b)
            packet = packet_ref[16 * m + b]
            side = l % 2
            across = packet.T[:BW]
            both = jnp.concatenate([across, across], axis=1)
            placed = jnp.where(lane // BW == side, both, 0.0)
            spot = (c, slice(None), pl.ds(pl.multiple_of(b // 8 * EP + l // 2 * 128, 128), 128))
            spread[spot] = spread[spot] + placed
            squares = jnp.where(lane >= BW, packet, pltpu.roll(packet, BW, 1))
            squares = jnp.where(lane // BW == side, squares, 0.0)
            rows = pl.ds(pl.multiple_of(l * BW, BW), BW)
            if b < 8:
                spot = (rows, pl.ds(pl.multiple_of(l // 2 * 128, 128), 128))
                front[spot] = front[spot] + squares
            else:
                spot = (m, l // 2, rows, slice(None))
                private[spot] = private[spot] + squares

        def split_spread(c, carry):
            high, low = halves(spread[c])
            spread_high[c] = high
            spread_low[c] = low
            return carry

        lax.fori_loop(0, NB, split_spread, 0)
        for b in range(16):
            c, l = numbers(32 * core + 16 * m + b)
            left = left_parts(packet_ref[16 * m + b][:, :BW])
            rows = pl.ds(pl.multiple_of(l * BW, BW), BW)
            begin = 0 if b < 8 else EP
            high = spread_high[c, :, begin:]
            taken = mm(left, jnp.concatenate([high, high, spread_low[c, :, begin:]], axis=0))
            if b < 8:
                front[rows, 0:EP] = front[rows, 0:EP] - taken[:, :EP]
                front[rows, EP * (1 + m):EP * (2 + m)] = front[rows, EP * (1 + m):EP * (2 + m)] - taken[:, EP:]
            else:
                for n in range(5):
                    private[m, n, rows, :] = private[m, n, rows, :] - taken[:, 128 * n:128 * n + 128]

    eliminate([front])
    for j in range(5):
        for i in range(10):
            rows21[j, 128 * i:128 * i + 128, :] = front[128 * j:128 * j + 128, EP + 128 * i:EP + 128 * i + 128].T
        for i in range(j, 5):
            rows11[j, 128 * i:128 * i + 128, :] = front[128 * j:128 * j + 128, 128 * i:128 * i + 128].T
        for i in range(j):
            rows11[j, 128 * i:128 * i + 128, :] = jnp.zeros((128, 128), f32)
    for w, who in enumerate((place, sibling)):
        spot1 = who % 8
        for n in range(0, EP, 128):
            rows_ref[w, 0, :, n:n + 128] = rows11[n // 128, pl.ds(spot1, 72, stride=8), :]
            rows_ref[w, 1, :, n:n + 128] = rows21[n // 128, pl.ds(spot1, 72, stride=8), :]
            rows_ref[w, 2, :, n:n + 128] = rows21[n // 128, pl.ds(EP + spot1, 72, stride=8), :]
    for n in range(0, EP, 128):
        some = [rows21[n // 128, pl.ds(EP + who, 40, stride=16), :] for who in (place, sibling)]
        high, low = halves(jnp.concatenate([rows21[n // 128, 0:E, :]] + some, axis=0))
        left_all[:, n:n + 128] = high
        left_all[:, EP + n:EP + n + 128] = low
        left_all[:, 2 * EP + n:2 * EP + n + 128] = high
    for n0, n1 in ((0, 256), (256, 512), (512, 640), (640, 896), (896, 1152), (1152, 1280)):
        high, low = halves(front[:, EP + n0:EP + n1])
        taken = mm(left_all[...], jnp.concatenate([high, high, low], axis=0))
        for n in range(n0, n1, 128):
            piece = taken[:, n - n0:n - n0 + 128]
            if n0 < EP:
                front_out[:, n:n + 128] = private[0, n // 128, 0:E, :] - piece[:E]
            else:
                front_out[:, n:n + 128] = -piece[:E]
            for w, who in enumerate((place, sibling)):
                own_rows = piece[E + 40 * w:E + 40 * w + 40]
                if n0 < EP:
                    own_out[w, :, n:n + 128] = -own_rows
                else:
                    own_out[w, :, n:n + 128] = private[1, (n - EP) // 128, pl.ds(who, 40, stride=16), :] - own_rows


def swap_kernel(front_ref, own_ref, rows_ref, front_in, own_in, rows_in, send, recv):
    greet((2,))
    pairs = [(rows_ref.at[1], rows_in), (own_ref.at[1], own_in)]
    for n in range(3):
        part = slice(192 * n, 192 * n + 192)
        pairs.append((front_ref.at[part, :], front_in.at[part, :]))
    copies = [
        pltpu.make_async_remote_copy(
            src, dst, send.at[n], recv.at[n], device_id=peer(2), device_id_type=MESH
        )
        for n, (src, dst) in enumerate(pairs)
    ]
    for copy in copies:
        copy.start()
    for copy in copies:
        copy.wait()


def top_kernel(
    early_ref, rows_ref, rows_in, front_ref, front_in, own_ref, own_in, out_ref, top_ref, front, rows11, own, stage
):
    place = group_place()
    core = place // 2 % 2
    here = core == place // 8
    for h in range(3):
        stage[h, 0:144, :] = early_ref[h]
        stage[h, 144:216, :] = jnp.where(here, rows_ref[0, h], rows_in[h])

    def finish(r):
        wide = min(128, 252 - r)
        for h in range(3):
            for n in range(0, E, 128):
                tall = min(128, E - n)
                out_ref[h, n:n + tall, r:r + wide] = stage[h, r:r + 128, n:n + 128].T[:tall, :wide]

    finish(0)
    front[E:EP, :] = jnp.zeros((EP - E, WIDE), f32)
    own[...] = jnp.zeros(own.shape, f32)
    front[0:E, 0:EP] = front_ref[:, 0:EP] + front_in[:, 0:EP]
    for side, matrix, few in ((core, front_ref, own_ref.at[0]), (1 - core, front_in, own_in)):
        lanes = pl.ds(pl.multiple_of(EP * (1 + side), 128), EP)
        rows = pl.ds(pl.multiple_of(40 * side, 8), 40)
        front[0:E, lanes] = matrix[:, EP:]
        own[rows, 0:EP] = few[:, 0:EP]
        own[rows, lanes] = few[:, EP:]
    eliminate([front], own)
    for j in range(5):
        for i in range(j, 5):
            rows11[j, 128 * i:128 * i + 128, :] = front[128 * j:128 * j + 128, 128 * i:128 * i + 128].T
        for i in range(j):
            rows11[j, 128 * i:128 * i + 128, :] = jnp.zeros((128, 128), f32)
    for n in range(0, EP, 128):
        stage[0, 216:252, n:n + 128] = rows11[n // 128, pl.ds(place, 36, stride=16), :]
    for h in range(2):
        stage[1 + h, 216:252, :] = own[40 * h:40 * h + 36, 0:EP]
        top_ref[h, :, 0:E] = own[40 * h:40 * h + 36, EP:EP + E]
        top_ref[h, :, E:2 * E] = own[40 * h:40 * h + 36, 2 * EP:2 * EP + E]
    finish(128)


VMEM = pl.BlockSpec(memory_space=pltpu.VMEM)
SMEM = pl.BlockSpec(memory_space=pltpu.SMEM)


PARAMS = pltpu.CompilerParams(vmem_limit_bytes=56 * 2**20)
FRONT = jax.ShapeDtypeStruct((E, 2 * EP), f32)


def groups(ids, raw, factors, last):
    return pl.pallas_call(
        groups_kernel,
        out_shape=(
            jax.ShapeDtypeStruct((3, 144, EP), f32),
            jax.ShapeDtypeStruct((2, 3, 72, EP), f32),
            FRONT,
            jax.ShapeDtypeStruct((2, 40, 2 * EP), f32),
        ),
        in_specs=[SMEM, VMEM, VMEM, VMEM],
        out_specs=(VMEM,) * 4,
        scratch_shapes=[
            pltpu.VMEM((EP, WIDE), f32),
            pltpu.VMEM((2, 5, EP, 128), f32),
            pltpu.VMEM((NB, BW, 2 * EP), f32),
            pltpu.VMEM((NB, BW, 2 * EP), bf16),
            pltpu.VMEM((NB, BW, 2 * EP), bf16),
            pltpu.VMEM((5, 2 * EP, 128), f32),
            pltpu.VMEM((5, EP, 128), f32),
            pltpu.VMEM((E + 80, WIDE), bf16),
            pltpu.VMEM((32, BW, 128), f32),
            pltpu.VMEM((3 * NB, BW, 3 * BW), bf16),
        ],
        compiler_params=PARAMS,
    )(ids, raw, factors, last)


def swap(front, own, rows):
    dma = pltpu.SemaphoreType.DMA
    return pl.pallas_call(
        swap_kernel,
        out_shape=(
            FRONT,
            jax.ShapeDtypeStruct((40, 2 * EP), f32),
            jax.ShapeDtypeStruct((3, 72, EP), f32),
        ),
        in_specs=[VMEM] * 3,
        out_specs=(VMEM,) * 3,
        scratch_shapes=[dma((5,)), dma((5,))],
        compiler_params=pltpu.CompilerParams(
            collective_id=1, has_side_effects=True, vmem_limit_bytes=40 * 2**20
        ),
    )(front, own, rows)


def top(early, rows, rows_in, front, front_in, own, own_in):
    return pl.pallas_call(
        top_kernel,
        out_shape=(jax.ShapeDtypeStruct((3, E, 252), f32), jax.ShapeDtypeStruct((2, 36, 2 * E), f32)),
        in_specs=[VMEM] * 7,
        out_specs=(VMEM, VMEM),
        scratch_shapes=[
            pltpu.VMEM((EP, WIDE), f32),
            pltpu.VMEM((5, EP, 128), f32),
            pltpu.VMEM((80, WIDE), f32),
            pltpu.VMEM((3, 256, EP), f32),
        ],
        compiler_params=PARAMS,
    )(early, rows, rows_in, front, front_in, own, own_in)


def exchange(cameras, landmarks, tiles):
    dma = pltpu.SemaphoreType.DMA
    return pl.pallas_call(
        exchange_kernel,
        out_shape=(
            jax.ShapeDtypeStruct((PEERS, 4, BW, 128), f32),
            jax.ShapeDtypeStruct((PEERS, BW, 128), f32),
            jax.ShapeDtypeStruct((4, BW // 2, 128), f32),
            jax.ShapeDtypeStruct((PEERS, 8, 128), jnp.int32),
        ),
        in_specs=[SMEM, SMEM, VMEM],
        out_specs=(VMEM, VMEM, VMEM, VMEM),
        scratch_shapes=[
            pltpu.VMEM((2, BW, 128), f32),
            pltpu.VMEM((4, 2, BW, 128), f32),
            pltpu.VMEM((BW, 128), f32),
            pltpu.VMEM((BW // 2, 128), f32),
            dma((4,)), dma((4,)), dma((PEERS,)), dma((PEERS,)),
            dma((9,)), dma((9,)), dma((10,)), dma((10,)),
            dma((PEERS,)), dma((PEERS,)), dma((PEERS,)), dma((3,)), dma((3,)),
        ],
        compiler_params=pltpu.CompilerParams(collective_id=0, has_side_effects=True),
    )(cameras, landmarks, tiles)


def local(jacobian, camera_block, landmark_block):
    blocks = jacobian[0]
    tiles = jnp.einsum("nrc,nrd->ncd", blocks, blocks, preferred_element_type=f32)
    raw, factors, last, ids = exchange(camera_block, landmark_block, tiles)
    early, rows, front, own = groups(ids, raw, factors, last)
    front_in, own_in, rows_in = swap(front, own, rows)
    factor_rows, top_rows = top(early, rows, rows_in, front, front_in, own, own_in)
    return factor_rows.transpose(0, 2, 1)[:, None], top_rows[:, None]


def solution(mesh):
    placed = (P("sub", "lm", None, None), P("sub", "lm"), P("sub", "lm"))
    return jax.shard_map(
        local,
        mesh=mesh,
        in_specs=placed,
        out_specs=(P(None, ("sub", "lm"), None, None), P(None, ("sub", "lm"), None, None)),
        check_vma=False,
    )
```

```python
import jax
import jax.numpy as jnp
from jax import lax
from jax.experimental import pallas as pl
from jax.experimental.pallas import tpu as pltpu
from jax.sharding import PartitionSpec as P

BW = 64
E = 576
NB = E // BW
EP = 640
WIDE = 3 * EP
PEERS = 16
MESH = pl.DeviceIdType.MESH
f32 = jnp.float32
bf16 = jnp.bfloat16


def lane_ids(shape):
    return lax.broadcasted_iota(jnp.int32, shape, 1)


def row_ids(shape):
    return lax.broadcasted_iota(jnp.int32, shape, 0)


def over_lanes(tile, column):
    return jnp.broadcast_to(tile[:, column : column + 1], tile.shape)


def over_rows(tile, row):
    return jnp.broadcast_to(tile[row : row + 1, :], tile.shape)


def factor_blocks(blocks):
    sub = row_ids((8, 128))
    mats = [[block[8 * i : 8 * i + 8, :] for i in range(8)] for block in blocks]
    for s in range(8):
        cols = [[[over_lanes(m[i], 8 * s + t) for i in range(s, 8)] for t in range(8)] for m in mats]
        pivots = [jnp.zeros((8, 128), f32) for _ in mats]
        for t in range(8):
            for b, m in enumerate(mats):
                row = over_rows(m[s], t)
                pivot = over_rows(cols[b][t][0], t)
                inverse = 1.0 / pivot
                pivots[b] = jnp.where(sub == t, pivot, pivots[b])
                scaled = [c * inverse for c in cols[b][t]]
                scaled[0] = jnp.where(sub > t, scaled[0], 0.0)
                for i in range(s, 8):
                    m[i] = m[i] - scaled[i - s] * row
                for u in range(t + 1, 8):
                    across = over_rows(cols[b][u][0], t)
                    for i in range(8 - s):
                        cols[b][u][i] = cols[b][u][i] - scaled[i] * across
        for b, m in enumerate(mats):
            m[s] = m[s] * lax.rsqrt(pivots[b])
    return [jnp.concatenate(m, axis=0) for m in mats]


def halves(value):
    high = value.astype(bf16)
    return high, (value - high.astype(f32)).astype(bf16)


def left_parts(value):
    high = value.astype(bf16).astype(f32)
    both = jnp.concatenate([high, value - high], axis=1).astype(bf16)
    return jnp.concatenate([both, high.astype(bf16)], axis=1)


def right_lanes(value):
    high = value.astype(bf16).astype(f32)
    both = jnp.concatenate([high, high], axis=1).astype(bf16)
    return jnp.concatenate([both, (value - high).astype(bf16)], axis=1)


def right_parts(value):
    high, low = halves(value)
    return jnp.concatenate([high, high, low], axis=0)


def mm(left, right):
    return jnp.dot(left, right, preferred_element_type=f32)


def mm_nt(left, right):
    return lax.dot_general(left, right, (((1,), (1,)), ((), ())), preferred_element_type=f32)


def group_place():
    return (lax.axis_index("sub") % 8) * 2 + lax.axis_index("lm")


def peer(mask):
    sub, lm = lax.axis_index("sub"), lax.axis_index("lm")
    step = mask // 2
    for bit in (1, 2, 4):
        if step & bit:
            sub = sub + bit - 2 * bit * ((sub // bit) % 2)
    if mask & 1:
        lm = 1 - lm
    return (sub, lm)


def relative(place, mask):
    for bit in (1, 2, 4, 8):
        if mask & bit:
            place = place + bit - 2 * bit * ((place // bit) % 2)
    return place


def greet(masks):
    barrier = pltpu.get_barrier_semaphore()
    for mask in masks:
        pl.semaphore_signal(barrier, inc=1, device_id=peer(mask), device_id_type=MESH)
    pl.semaphore_wait(barrier, len(masks))


ACROSS = (1, 5, 8, 9, 13, 4, 12)
FIRST, SECOND = slice(0, 2), slice(2, 4)
WHOLE = slice(0, 4)
PIECES = {
    "near": (1, WHOLE), "wrap": (5, WHOLE), "row": (8, WHOLE), "far_a": (4, FIRST), "far_b": (4, SECOND),
    "row_near": (9, WHOLE), "row_wrap": (13, WHOLE), "row_far_a": (12, FIRST), "row_far_b": (12, SECOND),
}
NAMES = tuple(PIECES)


def exchange_kernel(
    cam_ref, lmk_ref, tiles_ref, raw_ref, fac_ref, last_ref, ids_ref,
    cams_own, cams, fac_own, last_own,
    cam_send, cam_recv, id_send, id_recv, raw_send, raw_recv, pass_send, pass_recv,
    fac_send, fac_recv, fac_pass, last_send, last_recv,
):
    place = group_place()
    greet(range(1, PEERS))
    lane = lane_ids((BW, 128))
    row = row_ids((BW, 128))

    def remote(src, dst, send, recv, mask):
        return pltpu.make_async_remote_copy(src, dst, send, recv, device_id=peer(mask), device_id_type=MESH)

    for b in range(2):
        cams_own[b] = jnp.where(
            lane < BW, tiles_ref[2 * b, 0:BW, :], pltpu.roll(tiles_ref[2 * b + 1, 0:BW, :], BW, 1)
        )
    for b in range(4):
        ids_ref[pl.ds(place, 1), b:b + 1, :] = jnp.full((1, 1, 128), cam_ref[0, b], jnp.int32)
        ids_ref[pl.ds(place, 1), 4 + b:5 + b, :] = jnp.full((1, 1, 128), lmk_ref[0, b], jnp.int32)
    quick = [remote(cams_own, cams.at[place % 4], cam_send.at[mask], cam_recv.at[mask], mask) for mask in (3, 1, 2)]
    numbers = {
        mask: remote(ids_ref.at[place], ids_ref.at[place], id_send.at[mask], id_recv.at[mask], mask)
        for mask in (3, 1, 2) + tuple(range(4, PEERS))
    }
    for copy in quick:
        copy.start()
    for copy in numbers.values():
        copy.start()
    started = quick + list(numbers.values())

    own_tiles = tiles_ref.at[:, BW:2 * BW, :]
    arrivals = {}

    def piece(name, source, mask):
        at = NAMES.index(name)
        owner, part = PIECES[name]
        source_place = relative(relative(place, mask), owner)
        copy = remote(source, raw_ref.at[source_place, part], raw_send.at[at], raw_recv.at[at], mask)
        copy.start()
        arrivals[name] = copy

    piece("near", own_tiles, 1)
    piece("wrap", own_tiles, 5)
    piece("row", own_tiles, 8)
    to_core = []

    def share(at, source, slot):
        copy = remote(source, slot, pass_send.at[at], pass_recv.at[at], 2)
        copy.start()
        to_core.append(copy)

    def landed(name):
        arrivals[name].wait_recv()
        owner, part = PIECES[name]
        slot = raw_ref.at[relative(place, owner), part]
        share(NAMES.index(name), slot, slot)
        return slot

    share(len(NAMES), own_tiles, raw_ref.at[place])
    raw_ref[pl.ds(place, 1)] = tiles_ref[:, BW:2 * BW, :][None]
    cams[pl.ds(place % 4, 1)] = cams_own[...][None]

    for copy in quick:
        copy.wait_recv()
    for mask in (3, 1, 2):
        numbers[mask].wait_recv()
    quarter = place % 4
    start = jnp.where(lane == row, 2.0, jnp.where(lane == row + BW, 1.0, 0.0)).astype(f32)
    totals = [start, start, start]
    wanted = (quarter, quarter + 4, 8)
    for d in range(4):
        device = place - quarter + d
        for b in range(4):
            packed = cams[d, b // 2]
            if b % 2:
                packed = pltpu.roll(packed, BW, 1)
            packed = jnp.where(lane < BW, packed, 0.0)
            number = ids_ref[pl.ds(device, 1), b:b + 1, :].reshape(1, 128)
            for u in range(3):
                totals[u] = totals[u] + jnp.where(number == wanted[u], packed, 0.0)

    for name, mask in (("near", 5), ("wrap", 1), ("row", 1)):
        slot = landed(name)
        if name == "near":
            piece("far_a", slot.at[FIRST], 5)
        elif name == "wrap":
            piece("far_b", slot.at[SECOND], 1)
        else:
            piece("row_near", slot, 1)
            piece("row_wrap", slot, 5)

    mixed = []
    for block in factor_blocks(totals):
        mixed.append(jnp.where(lane >= row, block, pltpu.roll(block, BW, 1)))
    fac_own[...] = jnp.where(lane < BW, mixed[0], pltpu.roll(mixed[1], BW, 1))
    half = BW // 2
    last = jnp.concatenate([mixed[2][:half, :BW], mixed[2][half:, :BW]], axis=1)
    last_own[...] = last
    facs = {}
    for mask in ACROSS + (2,):
        facs[mask] = remote(fac_own, fac_ref.at[place], fac_send.at[mask], fac_recv.at[mask], mask)
        facs[mask].start()
    lasts = []
    for n, mask in enumerate((4, 8, 12)):
        copy = remote(last_own, last_ref.at[place // 4], last_send.at[n], last_recv.at[n], mask)
        copy.start()
        lasts.append(copy)
    fac_ref[pl.ds(place, 1)] = fac_own[...][None]
    last_ref[pl.ds(place // 4, 1)] = last[None]

    piece("row_far_a", landed("far_a"), 8)
    piece("row_far_b", landed("far_b"), 8)
    landed("row_near")
    landed("row_wrap")
    passed = []
    for mask in ACROSS:
        facs[mask].wait_recv()
        slot = fac_ref.at[relative(place, mask)]
        copy = remote(slot, slot, fac_pass.at[mask], fac_recv.at[mask ^ 2], 2)
        copy.start()
        passed.append(copy)
    landed("row_far_a")
    landed("row_far_b")
    facs[2].wait_recv()
    for copy in passed + lasts + to_core:
        copy.wait()
    for mask in range(4, PEERS):
        numbers[mask].wait_recv()
    for copy in started + list(facs.values()) + list(arrivals.values()):
        copy.wait_send()


def eliminate(fronts, own=None, finished=None):
    lane = lane_ids((BW, 128))
    row = row_ids((BW, 128))
    unit = jnp.where(lane == row + BW, 1.0, 0.0).astype(f32)
    diag = [front[0:BW, 0:128] for front in fronts]
    for k in range(NB):
        r0, t0 = BW * k, k // 2 * 128
        r1, t1 = r0 + BW, (k + 1) // 2 * 128
        if k % 2:
            diag = [pltpu.roll(tile, BW, 1) for tile in diag]
        done = factor_blocks([jnp.where(lane < BW, tile, unit) for tile in diag])
        following = []
        for front, block in zip(fronts, done):
            inverse = pltpu.roll(block, BW, 1)[:, :BW]
            upper = mm(left_parts(inverse), right_parts(front[r0:r1, t0:WIDE]))
            corner = jnp.where(jnp.logical_and(lane >= row, lane < BW), block, 0.0)
            if k % 2:
                first = pltpu.roll(corner, BW, 1)
            else:
                first = jnp.where(lane < BW, corner, upper[:, :128])
            front[r0:r1, t0:t0 + 128] = first
            front[r0:r1, t0 + 128:WIDE] = upper[:, 128:]
            high, low = halves(upper)
            parts = jnp.concatenate([high, high, low], axis=0)
            left = None
            if k < NB - 1:
                turned = upper[:, t1 - t0:EP - t0].T
                left = left_parts(turned[r1 - t1:E - t1])
                following.append(front[r1:r1 + BW, t1:t1 + 128] - mm(left[:BW], parts[:, t1 - t0:t1 - t0 + 128]))
            if own is not None:
                block_lanes = own[:, r0:r1]
                own_solved = mm_nt(left_parts(block_lanes), right_lanes(inverse))
                own_left = left_parts(own_solved)
            begin = t1 if k < NB - 1 else EP
            bounds = [n for n in (0, 256, 512, 640, 896, 1152, 1408, 1664, 1920) if n > begin]
            for n1 in bounds:
                n0 = begin
                begin = n1
                last = min(E, n1)
                piece = parts[:, n0 - t0:n1 - t0]
                if left is not None:
                    front[r1:last, n0:n1] = front[r1:last, n0:n1] - mm(left[:last - r1], piece)
                if own is not None:
                    own[:, n0:n1] = own[:, n0:n1] - mm(own_left, piece)
            if own is not None:
                own[:, r0:r1] = own_solved
        if finished is not None and (k % 2 or k == NB - 1):
            finished(k // 2)
        diag = following


def groups_kernel(
    ids_ref, raw_ref, fac_ref, last_ref, early_ref, rows_ref, front_out, own_out,
    front, private, spread, spread_high, spread_low, rows21, rows11, left_all, packet_ref, solver,
):
    place = group_place()
    core = place // 2 % 2
    sibling = place + 2 - 4 * core
    pair = place // 4
    lane = lane_ids((BW, 128))
    row = row_ids((BW, 128))

    def clear(ref, first, count, width):
        def step(i, carry):
            ref[pl.ds(pl.multiple_of(first + i * BW, BW), BW), :] = jnp.zeros((BW, width), f32)
            return carry

        lax.fori_loop(0, count // BW, step, 0)

    clear(front, 0, EP, WIDE)
    for m in range(2):
        for n in range(5):
            clear(private.at[m, n], 0, EP, 128)
    for h in range(3):
        early_ref[h] = jnp.zeros((144, EP), f32)
    for i in range(NB):
        spot = jnp.where(lane == row + BW * (i % 2), 1.0, 0.0).astype(f32)
        front[BW * i:BW * i + BW, i // 2 * 128:i // 2 * 128 + 128] = 2.0 * spot
        for m in range(2):
            private[m, i // 2, BW * i:BW * i + BW, :] = spot

    def numbers(j):
        return ids_ref[j // 4, j % 4, 0], ids_ref[j // 4, 4 + j % 4, 0] - NB

    def camera_factor(p, c):
        if c < 8:
            both = fac_ref[4 * p + c % 4]
            return pltpu.roll(both, BW, 1) if c >= 4 else both
        both = last_ref[p]
        return jnp.concatenate([both, pltpu.roll(both, BW, 1)], axis=0)

    for u, p in enumerate((2 * core, 2 * core + 1, pair)):
        for c in range(NB):
            turned = camera_factor(p, c).T[:BW]
            below = lane_ids((BW, BW)) - row_ids((BW, BW))
            solver[NB * u + c] = right_parts(jnp.where(below > 0, turned, jnp.where(below == 0, 1.0 / turned, 0.0)))
            if u == 2:
                rows11[c // 2, BW * c:BW * c + BW, c % 2 * BW:c % 2 * BW + BW] = jnp.where(below <= 0, turned, 0.0)
    for j in range(32):
        c, _ = numbers(32 * core + j)
        raw = raw_ref[8 * core + j // 4, j % 4]
        solved = mm(left_parts(raw[:, :BW]), solver[NB * (j // 16) + c])
        packet_ref[j] = jnp.where(lane < BW, jnp.concatenate([solved, solved], axis=1), raw)

    quarter = place % 4
    few = lane_ids((16, 128))
    for b in range(16):
        c, l = numbers(pair * 16 + b)
        raw = raw_ref[4 * pair + b // 4, b % 4, pl.ds(quarter, 16, stride=4), :]
        solved = mm(left_parts(raw[:, :BW]), solver[2 * NB + c])
        placed = jnp.where(few // BW == c % 2, jnp.concatenate([solved, solved], axis=1), 0.0)
        spot = (1 + b // 8, pl.ds(pl.multiple_of(l * 16, 16), 16), pl.ds(pl.multiple_of(c // 2 * 128, 128), 128))
        early_ref[spot] = early_ref[spot] + placed
    for c in range(NB):
        few_rows = rows11[c // 2, pl.ds(BW * c + quarter, 16, stride=4), :]
        early_ref[0, 16 * c:16 * c + 16, c // 2 * 128:c // 2 * 128 + 128] = jnp.where(few // BW == c % 2, few_rows, 0.0)

    for m in range(2):

        def clear_spread(c, carry):
            spread[c] = jnp.zeros((BW, 2 * EP), f32)
            return carry

        lax.fori_loop(0, NB, clear_spread, 0)
        for b in range(16):
            c, l = numbers(32 * core + 16 * m + b)
            packet = packet_ref[16 * m + b]
            side = l % 2
            across = packet.T[:BW]
            both = jnp.concatenate([across, across], axis=1)
            placed = jnp.where(lane // BW == side, both, 0.0)
            spot = (c, slice(None), pl.ds(pl.multiple_of(b // 8 * EP + l // 2 * 128, 128), 128))
            spread[spot] = spread[spot] + placed
            squares = jnp.where(lane >= BW, packet, pltpu.roll(packet, BW, 1))
            squares = jnp.where(lane // BW == side, squares, 0.0)
            rows = pl.ds(pl.multiple_of(l * BW, BW), BW)
            if b < 8:
                spot = (rows, pl.ds(pl.multiple_of(l // 2 * 128, 128), 128))
                front[spot] = front[spot] + squares
            else:
                spot = (m, l // 2, rows, slice(None))
                private[spot] = private[spot] + squares

        def split_spread(c, carry):
            high, low = halves(spread[c])
            spread_high[c] = high
            spread_low[c] = low
            return carry

        lax.fori_loop(0, NB, split_spread, 0)
        for b in range(16):
            c, l = numbers(32 * core + 16 * m + b)
            left = left_parts(packet_ref[16 * m + b][:, :BW])
            rows = pl.ds(pl.multiple_of(l * BW, BW), BW)
            begin = 0 if b < 8 else EP
            high = spread_high[c, :, begin:]
            taken = mm(left, jnp.concatenate([high, high, spread_low[c, :, begin:]], axis=0))
            if b < 8:
                front[rows, 0:EP] = front[rows, 0:EP] - taken[:, :EP]
                front[rows, EP * (1 + m):EP * (2 + m)] = front[rows, EP * (1 + m):EP * (2 + m)] - taken[:, EP:]
            else:
                for n in range(5):
                    private[m, n, rows, :] = private[m, n, rows, :] - taken[:, 128 * n:128 * n + 128]

    def product(first, end):
        lanes = slice(128 * first, 128 * end)
        high = left_all[:, lanes]
        left = jnp.concatenate([high, left_all[:, EP + 128 * first:EP + 128 * end], high], axis=1)
        for n0, n1 in ((0, 256), (256, 512), (512, 640), (640, 896), (896, 1152), (1152, 1280)):
            high, low = halves(front[lanes, EP + n0:EP + n1])
            taken = mm(left, jnp.concatenate([high, high, low], axis=0))
            for n in range(n0, n1, 128):
                piece = taken[:, n - n0:n - n0 + 128]
                tile = slice(n, n + 128)
                if first:
                    front_out[:, tile] = front_out[:, tile] - piece[:E]
                elif n0 < EP:
                    front_out[:, tile] = private[0, n // 128, 0:E, :] - piece[:E]
                else:
                    front_out[:, tile] = -piece[:E]
                for w, who in enumerate((place, sibling)):
                    own_rows = piece[E + 40 * w:E + 40 * w + 40]
                    if first:
                        own_out[w, :, tile] = own_out[w, :, tile] - own_rows
                    elif n0 < EP:
                        own_out[w, :, tile] = -own_rows
                    else:
                        own_out[w, :, tile] = private[1, (n - EP) // 128, pl.ds(who, 40, stride=16), :] - own_rows

    def finished(j):
        for i in range(10):
            rows21[j, 128 * i:128 * i + 128, :] = front[128 * j:128 * j + 128, EP + 128 * i:EP + 128 * i + 128].T
        for i in range(j, 5):
            rows11[j, 128 * i:128 * i + 128, :] = front[128 * j:128 * j + 128, 128 * i:128 * i + 128].T
        for i in range(j):
            rows11[j, 128 * i:128 * i + 128, :] = jnp.zeros((128, 128), f32)
        some = [rows21[j, pl.ds(EP + who, 40, stride=16), :] for who in (place, sibling)]
        high, low = halves(jnp.concatenate([rows21[j, 0:E, :]] + some, axis=0))
        left_all[:, 128 * j:128 * j + 128] = high
        left_all[:, EP + 128 * j:EP + 128 * j + 128] = low
        if j == 2:
            product(0, 3)

    eliminate([front], finished=finished)
    product(3, 5)
    for w, who in enumerate((place, sibling)):
        spot1 = who % 8
        for n in range(0, EP, 128):
            rows_ref[w, 0, :, n:n + 128] = rows11[n // 128, pl.ds(spot1, 72, stride=8), :]
            rows_ref[w, 1, :, n:n + 128] = rows21[n // 128, pl.ds(spot1, 72, stride=8), :]
            rows_ref[w, 2, :, n:n + 128] = rows21[n // 128, pl.ds(EP + spot1, 72, stride=8), :]


def swap_kernel(front_ref, own_ref, rows_ref, front_in, own_in, rows_in, send, recv):
    greet((2,))
    pairs = [(rows_ref.at[1], rows_in), (own_ref.at[1], own_in)]
    for n in range(3):
        part = slice(192 * n, 192 * n + 192)
        pairs.append((front_ref.at[part, :], front_in.at[part, :]))
    copies = [
        pltpu.make_async_remote_copy(
            src, dst, send.at[n], recv.at[n], device_id=peer(2), device_id_type=MESH
        )
        for n, (src, dst) in enumerate(pairs)
    ]
    for copy in copies:
        copy.start()
    for copy in copies:
        copy.wait()


def top_kernel(
    early_ref, rows_ref, rows_in, front_ref, front_in, own_ref, own_in, out_ref, top_ref, front, rows11, own, stage
):
    place = group_place()
    core = place // 2 % 2
    here = core == place // 8
    for h in range(3):
        stage[h, 0:144, :] = early_ref[h]
        stage[h, 144:216, :] = jnp.where(here, rows_ref[0, h], rows_in[h])

    def finish(r):
        wide = min(128, 252 - r)
        for h in range(3):
            for n in range(0, E, 128):
                tall = min(128, E - n)
                out_ref[h, n:n + tall, r:r + wide] = stage[h, r:r + 128, n:n + 128].T[:tall, :wide]

    front[E:EP, :] = jnp.zeros((EP - E, WIDE), f32)
    own[...] = jnp.zeros(own.shape, f32)
    front[0:E, 0:EP] = front_ref[:, 0:EP] + front_in[:, 0:EP]
    for side, matrix, few in ((core, front_ref, own_ref.at[0]), (1 - core, front_in, own_in)):
        lanes = pl.ds(pl.multiple_of(EP * (1 + side), 128), EP)
        rows = pl.ds(pl.multiple_of(40 * side, 8), 40)
        front[0:E, lanes] = matrix[:, EP:]
        own[rows, 0:EP] = few[:, 0:EP]
        own[rows, lanes] = few[:, EP:]

    def finished(j):
        for i in range(j, 5):
            rows11[j, 128 * i:128 * i + 128, :] = front[128 * j:128 * j + 128, 128 * i:128 * i + 128].T
        for i in range(j):
            rows11[j, 128 * i:128 * i + 128, :] = jnp.zeros((128, 128), f32)
        if j == 1:
            finish(0)

    eliminate([front], own, finished)
    for n in range(0, EP, 128):
        stage[0, 216:252, n:n + 128] = rows11[n // 128, pl.ds(place, 36, stride=16), :]
    for h in range(2):
        stage[1 + h, 216:252, :] = own[40 * h:40 * h + 36, 0:EP]
        wide = jnp.concatenate([own[40 * h:40 * h + 40, EP:EP + E], own[40 * h:40 * h + 40, 2 * EP:2 * EP + E]], axis=1)
        for i in range(36):
            top_ref[36 * h + i] = wide[i:i + 1, :]
    finish(128)


VMEM = pl.BlockSpec(memory_space=pltpu.VMEM)
SMEM = pl.BlockSpec(memory_space=pltpu.SMEM)


FRONT = jax.ShapeDtypeStruct((E, 2 * EP), f32)


def groups(ids, raw, factors, last):
    return pl.pallas_call(
        groups_kernel,
        out_shape=(
            jax.ShapeDtypeStruct((3, 144, EP), f32),
            jax.ShapeDtypeStruct((2, 3, 72, EP), f32),
            FRONT,
            jax.ShapeDtypeStruct((2, 40, 2 * EP), f32),
        ),
        in_specs=[SMEM, VMEM, VMEM, VMEM],
        out_specs=(VMEM,) * 4,
        scratch_shapes=[
            pltpu.VMEM((EP, WIDE), f32),
            pltpu.VMEM((2, 5, EP, 128), f32),
            pltpu.VMEM((NB, BW, 2 * EP), f32),
            pltpu.VMEM((NB, BW, 2 * EP), bf16),
            pltpu.VMEM((NB, BW, 2 * EP), bf16),
            pltpu.VMEM((5, 2 * EP, 128), f32),
            pltpu.VMEM((5, EP, 128), f32),
            pltpu.VMEM((E + 80, 2 * EP), bf16),
            pltpu.VMEM((32, BW, 128), f32),
            pltpu.VMEM((3 * NB, 3 * BW, BW), bf16),
        ],
        compiler_params=pltpu.CompilerParams(vmem_limit_bytes=32 * 2**20),
    )(ids, raw, factors, last)


def swap(front, own, rows):
    dma = pltpu.SemaphoreType.DMA
    return pl.pallas_call(
        swap_kernel,
        out_shape=(
            FRONT,
            jax.ShapeDtypeStruct((40, 2 * EP), f32),
            jax.ShapeDtypeStruct((3, 72, EP), f32),
        ),
        in_specs=[VMEM] * 3,
        out_specs=(VMEM,) * 3,
        scratch_shapes=[dma((5,)), dma((5,))],
        compiler_params=pltpu.CompilerParams(
            collective_id=1, has_side_effects=True, vmem_limit_bytes=4 * 2**20
        ),
    )(front, own, rows)


def top(early, rows, rows_in, front, front_in, own, own_in):
    return pl.pallas_call(
        top_kernel,
        out_shape=(jax.ShapeDtypeStruct((3, E, 252), f32), jax.ShapeDtypeStruct((72, 1, 2 * E), f32)),
        in_specs=[VMEM] * 7,
        out_specs=(VMEM, VMEM),
        scratch_shapes=[
            pltpu.VMEM((EP, WIDE), f32),
            pltpu.VMEM((5, EP, 128), f32),
            pltpu.VMEM((80, WIDE), f32),
            pltpu.VMEM((3, 256, EP), f32),
        ],
        compiler_params=pltpu.CompilerParams(vmem_limit_bytes=20 * 2**20),
    )(early, rows, rows_in, front, front_in, own, own_in)


def exchange(cameras, landmarks, tiles):
    dma = pltpu.SemaphoreType.DMA
    return pl.pallas_call(
        exchange_kernel,
        out_shape=(
            jax.ShapeDtypeStruct((PEERS, 4, BW, 128), f32),
            jax.ShapeDtypeStruct((PEERS, BW, 128), f32),
            jax.ShapeDtypeStruct((4, BW // 2, 128), f32),
            jax.ShapeDtypeStruct((PEERS, 8, 128), jnp.int32),
        ),
        in_specs=[SMEM, SMEM, VMEM],
        out_specs=(VMEM, VMEM, VMEM, VMEM),
        scratch_shapes=[
            pltpu.VMEM((2, BW, 128), f32),
            pltpu.VMEM((4, 2, BW, 128), f32),
            pltpu.VMEM((BW, 128), f32),
            pltpu.VMEM((BW // 2, 128), f32),
            dma((4,)), dma((4,)), dma((PEERS,)), dma((PEERS,)),
            dma((9,)), dma((9,)), dma((10,)), dma((10,)),
            dma((PEERS,)), dma((PEERS,)), dma((PEERS,)), dma((3,)), dma((3,)),
        ],
        compiler_params=pltpu.CompilerParams(
            collective_id=0, has_side_effects=True, vmem_limit_bytes=8 * 2**20
        ),
    )(cameras, landmarks, tiles)


def local(jacobian, camera_block, landmark_block):
    blocks = jacobian[0]
    tiles = jnp.einsum("nrc,nrd->ncd", blocks, blocks, preferred_element_type=f32)
    raw, factors, last, ids = exchange(camera_block, landmark_block, tiles)
    early, rows, front, own = groups(ids, raw, factors, last)
    front_in, own_in, rows_in = swap(front, own, rows)
    factor_rows, top_rows = top(early, rows, rows_in, front, front_in, own, own_in)
    return factor_rows.transpose(0, 2, 1)[:, None], top_rows.reshape(2, 36, 1, 2 * E).transpose(0, 2, 1, 3)


def solution(mesh):
    placed = (P("sub", "lm", None, None), P("sub", "lm"), P("sub", "lm"))
    return jax.shard_map(
        local,
        mesh=mesh,
        in_specs=placed,
        out_specs=(P(None, ("sub", "lm"), None, None), P(None, ("sub", "lm"), None, None)),
        check_vma=False,
    )
```

```python
import jax
import jax.numpy as jnp
from jax import lax
from jax.experimental import pallas as pl
from jax.experimental.pallas import tpu as pltpu
from jax.sharding import PartitionSpec as P

BW = 64
E = 576
NB = E // BW
EP = 640
WIDE = 3 * EP
PEERS = 16
MESH = pl.DeviceIdType.MESH
f32 = jnp.float32
bf16 = jnp.bfloat16


def lane_ids(shape):
    return lax.broadcasted_iota(jnp.int32, shape, 1)


def row_ids(shape):
    return lax.broadcasted_iota(jnp.int32, shape, 0)


def over_lanes(tile, column):
    return jnp.broadcast_to(tile[:, column : column + 1], tile.shape)


def over_rows(tile, row):
    return jnp.broadcast_to(tile[row : row + 1, :], tile.shape)


def factor_one(block):
    sub = row_ids((8, 128))
    m = [block[8 * i : 8 * i + 8, :] for i in range(8)]
    for s in range(8):
        cols = [[over_lanes(m[i], 8 * s + t) for i in range(s, 8)] for t in range(8)]
        pivots = jnp.zeros((8, 128), f32)
        for t in range(0, 8, 2):
            ca, cb = cols[t], cols[t + 1]
            first, cross, second = over_rows(ca[0], t), over_rows(cb[0], t), over_rows(cb[0], t + 1)
            det = first * second - cross * cross
            inverse = 1.0 / det
            first_inverse = 1.0 / first
            row_a, row_b = over_rows(m[s], t), over_rows(m[s], t + 1)
            pivots = jnp.where(sub == t, first, jnp.where(sub == t + 1, det * first_inverse, pivots))
            fa = [(x * second - y * cross) * inverse for x, y in zip(ca, cb)]
            fb = [(y * first - x * cross) * inverse for x, y in zip(ca, cb)]
            fa[0] = jnp.where(sub > t + 1, fa[0], jnp.where(sub == t + 1, cross * first_inverse, 0.0))
            fb[0] = jnp.where(sub > t + 1, fb[0], 0.0)
            for i in range(s, 8):
                m[i] = m[i] - (fa[i - s] * row_a + fb[i - s] * row_b)
            for u in range(t + 2, 8):
                xa, xb = over_rows(cols[u][0], t), over_rows(cols[u][0], t + 1)
                for i in range(8 - s):
                    cols[u][i] = cols[u][i] - (fa[i] * xa + fb[i] * xb)
        m[s] = m[s] * lax.rsqrt(pivots)
    return jnp.concatenate(m, axis=0)


def factor_blocks(blocks, midway=None):
    sub = row_ids((8, 128))
    mats = [[block[8 * i : 8 * i + 8, :] for i in range(8)] for block in blocks]
    for s in range(8):
        if s == 4 and midway is not None:
            midway()
        cols = [[[over_lanes(m[i], 8 * s + t) for i in range(s, 8)] for t in range(8)] for m in mats]
        pivots = [jnp.zeros((8, 128), f32) for _ in mats]
        for t in range(8):
            for b, m in enumerate(mats):
                row = over_rows(m[s], t)
                pivot = over_rows(cols[b][t][0], t)
                inverse = 1.0 / pivot
                pivots[b] = jnp.where(sub == t, pivot, pivots[b])
                scaled = [c * inverse for c in cols[b][t]]
                scaled[0] = jnp.where(sub > t, scaled[0], 0.0)
                for i in range(s, 8):
                    m[i] = m[i] - scaled[i - s] * row
                for u in range(t + 1, 8):
                    across = over_rows(cols[b][u][0], t)
                    for i in range(8 - s):
                        cols[b][u][i] = cols[b][u][i] - scaled[i] * across
        for b, m in enumerate(mats):
            m[s] = m[s] * lax.rsqrt(pivots[b])
    return [jnp.concatenate(m, axis=0) for m in mats]


def halves(value):
    high = value.astype(bf16)
    return high, (value - high.astype(f32)).astype(bf16)


def left_parts(value):
    high = value.astype(bf16).astype(f32)
    both = jnp.concatenate([high, value - high], axis=1).astype(bf16)
    return jnp.concatenate([both, high.astype(bf16)], axis=1)


def right_lanes(value):
    high = value.astype(bf16).astype(f32)
    both = jnp.concatenate([high, high], axis=1).astype(bf16)
    return jnp.concatenate([both, (value - high).astype(bf16)], axis=1)


def right_parts(value):
    high, low = halves(value)
    return jnp.concatenate([high, high, low], axis=0)


def mm(left, right):
    return jnp.dot(left, right, preferred_element_type=f32)


def mm_nt(left, right):
    return lax.dot_general(left, right, (((1,), (1,)), ((), ())), preferred_element_type=f32)


def group_place():
    return (lax.axis_index("sub") % 8) * 2 + lax.axis_index("lm")


def peer(mask):
    sub, lm = lax.axis_index("sub"), lax.axis_index("lm")
    step = mask // 2
    for bit in (1, 2, 4):
        if step & bit:
            sub = sub + bit - 2 * bit * ((sub // bit) % 2)
    if mask & 1:
        lm = 1 - lm
    return (sub, lm)


def relative(place, mask):
    for bit in (1, 2, 4, 8):
        if mask & bit:
            place = place + bit - 2 * bit * ((place // bit) % 2)
    return place


def greet(masks):
    barrier = pltpu.get_barrier_semaphore()
    for mask in masks:
        pl.semaphore_signal(barrier, inc=1, device_id=peer(mask), device_id_type=MESH)
    pl.semaphore_wait(barrier, len(masks))


ACROSS = (1, 5, 8, 9, 13, 4, 12)
FIRST, SECOND = slice(0, 2), slice(2, 4)
WHOLE = slice(0, 4)
PIECES = {
    "near": (1, WHOLE), "wrap": (5, WHOLE), "row": (8, WHOLE), "far_a": (4, FIRST), "far_b": (4, SECOND),
    "row_near": (9, WHOLE), "row_wrap": (13, WHOLE), "row_far_a": (12, FIRST), "row_far_b": (12, SECOND),
}
NAMES = tuple(PIECES)


def exchange_kernel(
    cam_ref, lmk_ref, tiles_ref, raw_ref, fac_ref, last_ref, ids_ref,
    cams_own, cams, fac_own, last_own,
    cam_send, cam_recv, id_send, id_recv, raw_send, raw_recv, pass_send, pass_recv,
    fac_send, fac_recv, fac_pass, last_send, last_recv,
):
    place = group_place()
    greet(range(1, PEERS))
    lane = lane_ids((BW, 128))
    row = row_ids((BW, 128))

    def remote(src, dst, send, recv, mask):
        return pltpu.make_async_remote_copy(src, dst, send, recv, device_id=peer(mask), device_id_type=MESH)

    for b in range(2):
        cams_own[b] = jnp.where(
            lane < BW, tiles_ref[2 * b, 0:BW, :], pltpu.roll(tiles_ref[2 * b + 1, 0:BW, :], BW, 1)
        )
    for b in range(4):
        ids_ref[pl.ds(place, 1), b:b + 1, :] = jnp.full((1, 1, 128), cam_ref[0, b], jnp.int32)
        ids_ref[pl.ds(place, 1), 4 + b:5 + b, :] = jnp.full((1, 1, 128), lmk_ref[0, b], jnp.int32)
    quick = [remote(cams_own, cams.at[place % 4], cam_send.at[mask], cam_recv.at[mask], mask) for mask in (3, 1, 2)]
    numbers = {
        mask: remote(ids_ref.at[place], ids_ref.at[place], id_send.at[mask], id_recv.at[mask], mask)
        for mask in (3, 1, 2) + tuple(range(4, PEERS))
    }
    for copy in quick:
        copy.start()
    for copy in numbers.values():
        copy.start()
    started = quick + list(numbers.values())

    own_tiles = tiles_ref.at[:, BW:2 * BW, :]
    arrivals = {}

    def piece(name, source, mask):
        at = NAMES.index(name)
        owner, part = PIECES[name]
        source_place = relative(relative(place, mask), owner)
        copy = remote(source, raw_ref.at[source_place, part], raw_send.at[at], raw_recv.at[at], mask)
        copy.start()
        arrivals[name] = copy

    piece("near", own_tiles, 1)
    piece("wrap", own_tiles, 5)
    piece("row", own_tiles, 8)
    to_core = []

    def share(at, source, slot):
        copy = remote(source, slot, pass_send.at[at], pass_recv.at[at], 2)
        copy.start()
        to_core.append(copy)

    def landed(name):
        arrivals[name].wait_recv()
        owner, part = PIECES[name]
        slot = raw_ref.at[relative(place, owner), part]
        share(NAMES.index(name), slot, slot)
        return slot

    share(len(NAMES), own_tiles, raw_ref.at[place])
    raw_ref[pl.ds(place, 1)] = tiles_ref[:, BW:2 * BW, :][None]
    cams[pl.ds(place % 4, 1)] = cams_own[...][None]

    for copy in quick:
        copy.wait_recv()
    for mask in (3, 1, 2):
        numbers[mask].wait_recv()
    quarter = place % 4
    start = jnp.where(lane == row, 2.0, jnp.where(lane == row + BW, 1.0, 0.0)).astype(f32)
    totals = [start, start, start]
    wanted = (quarter, quarter + 4, 8)
    for d in range(4):
        device = place - quarter + d
        for b in range(4):
            packed = cams[d, b // 2]
            if b % 2:
                packed = pltpu.roll(packed, BW, 1)
            packed = jnp.where(lane < BW, packed, 0.0)
            number = ids_ref[pl.ds(device, 1), b:b + 1, :].reshape(1, 128)
            for u in range(3):
                totals[u] = totals[u] + jnp.where(number == wanted[u], packed, 0.0)

    def forward():
        for name, mask in (("near", 5), ("wrap", 1), ("row", 1)):
            slot = landed(name)
            if name == "near":
                piece("far_a", slot.at[FIRST], 5)
            elif name == "wrap":
                piece("far_b", slot.at[SECOND], 1)
            else:
                piece("row_near", slot, 1)
                piece("row_wrap", slot, 5)

    mixed = []
    for block in factor_blocks(totals, forward):
        mixed.append(jnp.where(lane >= row, block, pltpu.roll(block, BW, 1)))
    fac_own[...] = jnp.where(lane < BW, mixed[0], pltpu.roll(mixed[1], BW, 1))
    half = BW // 2
    last = jnp.concatenate([mixed[2][:half, :BW], mixed[2][half:, :BW]], axis=1)
    last_own[...] = last
    facs = {}
    for mask in ACROSS + (2,):
        facs[mask] = remote(fac_own, fac_ref.at[place], fac_send.at[mask], fac_recv.at[mask], mask)
        facs[mask].start()
    lasts = []
    for n, mask in enumerate((4, 8, 12)):
        copy = remote(last_own, last_ref.at[place // 4], last_send.at[n], last_recv.at[n], mask)
        copy.start()
        lasts.append(copy)
    fac_ref[pl.ds(place, 1)] = fac_own[...][None]
    last_ref[pl.ds(place // 4, 1)] = last[None]

    piece("row_far_a", landed("far_a"), 8)
    piece("row_far_b", landed("far_b"), 8)
    landed("row_near")
    landed("row_wrap")
    passed = []
    for mask in ACROSS:
        facs[mask].wait_recv()
        slot = fac_ref.at[relative(place, mask)]
        copy = remote(slot, slot, fac_pass.at[mask], fac_recv.at[mask ^ 2], 2)
        copy.start()
        passed.append(copy)
    landed("row_far_a")
    landed("row_far_b")
    facs[2].wait_recv()
    for copy in passed + lasts + to_core:
        copy.wait()
    for mask in range(4, PEERS):
        numbers[mask].wait_recv()
    for copy in started + list(facs.values()) + list(arrivals.values()):
        copy.wait_send()


def eliminate(fronts, own=None, finished=None):
    lane = lane_ids((BW, 128))
    row = row_ids((BW, 128))
    unit = jnp.where(lane == row + BW, 1.0, 0.0).astype(f32)
    diag = [front[0:BW, 0:128] for front in fronts]
    for k in range(NB):
        r0, t0 = BW * k, k // 2 * 128
        r1, t1 = r0 + BW, (k + 1) // 2 * 128
        if k % 2:
            diag = [pltpu.roll(tile, BW, 1) for tile in diag]
        done = [factor_one(jnp.where(lane < BW, tile, unit)) for tile in diag]
        following = []
        for front, block in zip(fronts, done):
            inverse = pltpu.roll(block, BW, 1)[:, :BW]
            upper = mm(left_parts(inverse), right_parts(front[r0:r1, t0:WIDE]))
            corner = jnp.where(jnp.logical_and(lane >= row, lane < BW), block, 0.0)
            if k % 2:
                first = pltpu.roll(corner, BW, 1)
            else:
                first = jnp.where(lane < BW, corner, upper[:, :128])
            front[r0:r1, t0:t0 + 128] = first
            front[r0:r1, t0 + 128:WIDE] = upper[:, 128:]
            high, low = halves(upper)
            parts = jnp.concatenate([high, high, low], axis=0)
            left = None
            if k < NB - 1:
                turned = upper[:, t1 - t0:EP - t0].T
                left = left_parts(turned[r1 - t1:E - t1])
                following.append(front[r1:r1 + BW, t1:t1 + 128] - mm(left[:BW], parts[:, t1 - t0:t1 - t0 + 128]))
            if own is not None:
                block_lanes = own[:, r0:r1]
                own_solved = mm_nt(left_parts(block_lanes), right_lanes(inverse))
                own_left = left_parts(own_solved)
            begin = t1 if k < NB - 1 else EP
            bounds = [n for n in (0, 256, 512, 640, 896, 1152, 1408, 1664, 1920) if n > begin]
            for n1 in bounds:
                n0 = begin
                begin = n1
                last = min(E, n1)
                piece = parts[:, n0 - t0:n1 - t0]
                if left is not None:
                    front[r1:last, n0:n1] = front[r1:last, n0:n1] - mm(left[:last - r1], piece)
                if own is not None:
                    own[:, n0:n1] = own[:, n0:n1] - mm(own_left, piece)
            if own is not None:
                own[:, r0:r1] = own_solved
        if finished is not None and (k % 2 or k == NB - 1):
            finished(k // 2)
        diag = following


def groups_kernel(
    ids_ref, raw_ref, fac_ref, last_ref, early_ref, rows_ref, front_out, own_out,
    front, private, spread, spread_high, spread_low, rows21, rows11, left_all, packet_ref, solver,
):
    place = group_place()
    core = place // 2 % 2
    sibling = place + 2 - 4 * core
    pair = place // 4
    lane = lane_ids((BW, 128))
    row = row_ids((BW, 128))

    def clear(ref, first, count, width):
        def step(i, carry):
            ref[pl.ds(pl.multiple_of(first + i * BW, BW), BW), :] = jnp.zeros((BW, width), f32)
            return carry

        lax.fori_loop(0, count // BW, step, 0)

    clear(front, 0, EP, WIDE)
    for m in range(2):
        for n in range(5):
            clear(private.at[m, n], 0, EP, 128)
    for h in range(3):
        early_ref[h] = jnp.zeros((144, EP), f32)
    for i in range(NB):
        spot = jnp.where(lane == row + BW * (i % 2), 1.0, 0.0).astype(f32)
        front[BW * i:BW * i + BW, i // 2 * 128:i // 2 * 128 + 128] = 2.0 * spot
        for m in range(2):
            private[m, i // 2, BW * i:BW * i + BW, :] = spot

    def numbers(j):
        return ids_ref[j // 4, j % 4, 0], ids_ref[j // 4, 4 + j % 4, 0] - NB

    def camera_factor(p, c):
        if c < 8:
            both = fac_ref[4 * p + c % 4]
            return pltpu.roll(both, BW, 1) if c >= 4 else both
        both = last_ref[p]
        return jnp.concatenate([both, pltpu.roll(both, BW, 1)], axis=0)

    for u, p in enumerate((2 * core, 2 * core + 1, pair)):
        for c in range(NB):
            turned = camera_factor(p, c).T[:BW]
            below = lane_ids((BW, BW)) - row_ids((BW, BW))
            solver[NB * u + c] = right_parts(jnp.where(below > 0, turned, jnp.where(below == 0, 1.0 / turned, 0.0)))
            if u == 2:
                rows11[c // 2, BW * c:BW * c + BW, c % 2 * BW:c % 2 * BW + BW] = jnp.where(below <= 0, turned, 0.0)
    for j in range(32):
        c, _ = numbers(32 * core + j)
        raw = raw_ref[8 * core + j // 4, j % 4]
        solved = mm(left_parts(raw[:, :BW]), solver[NB * (j // 16) + c])
        packet_ref[j] = jnp.where(lane < BW, jnp.concatenate([solved, solved], axis=1), raw)

    quarter = place % 4
    few = lane_ids((16, 128))
    for b in range(16):
        c, l = numbers(pair * 16 + b)
        raw = raw_ref[4 * pair + b // 4, b % 4, pl.ds(quarter, 16, stride=4), :]
        solved = mm(left_parts(raw[:, :BW]), solver[2 * NB + c])
        placed = jnp.where(few // BW == c % 2, jnp.concatenate([solved, solved], axis=1), 0.0)
        spot = (1 + b // 8, pl.ds(pl.multiple_of(l * 16, 16), 16), pl.ds(pl.multiple_of(c // 2 * 128, 128), 128))
        early_ref[spot] = early_ref[spot] + placed
    for c in range(NB):
        few_rows = rows11[c // 2, pl.ds(BW * c + quarter, 16, stride=4), :]
        early_ref[0, 16 * c:16 * c + 16, c // 2 * 128:c // 2 * 128 + 128] = jnp.where(few // BW == c % 2, few_rows, 0.0)

    for m in range(2):

        def clear_spread(c, carry):
            spread[c] = jnp.zeros((BW, 2 * EP), f32)
            return carry

        lax.fori_loop(0, NB, clear_spread, 0)
        for b in range(16):
            c, l = numbers(32 * core + 16 * m + b)
            packet = packet_ref[16 * m + b]
            side = l % 2
            across = packet.T[:BW]
            both = jnp.concatenate([across, across], axis=1)
            placed = jnp.where(lane // BW == side, both, 0.0)
            spot = (c, slice(None), pl.ds(pl.multiple_of(b // 8 * EP + l // 2 * 128, 128), 128))
            spread[spot] = spread[spot] + placed
            squares = jnp.where(lane >= BW, packet, pltpu.roll(packet, BW, 1))
            squares = jnp.where(lane // BW == side, squares, 0.0)
            rows = pl.ds(pl.multiple_of(l * BW, BW), BW)
            if b < 8:
                spot = (rows, pl.ds(pl.multiple_of(l // 2 * 128, 128), 128))
                front[spot] = front[spot] + squares
            else:
                spot = (m, l // 2, rows, slice(None))
                private[spot] = private[spot] + squares

        def split_spread(c, carry):
            high, low = halves(spread[c])
            spread_high[c] = high
            spread_low[c] = low
            return carry

        lax.fori_loop(0, NB, split_spread, 0)
        for b in range(16):
            c, l = numbers(32 * core + 16 * m + b)
            left = left_parts(packet_ref[16 * m + b][:, :BW])
            rows = pl.ds(pl.multiple_of(l * BW, BW), BW)
            begin = 0 if b < 8 else EP
            high = spread_high[c, :, begin:]
            taken = mm(left, jnp.concatenate([high, high, spread_low[c, :, begin:]], axis=0))
            if b < 8:
                front[rows, 0:EP] = front[rows, 0:EP] - taken[:, :EP]
                front[rows, EP * (1 + m):EP * (2 + m)] = front[rows, EP * (1 + m):EP * (2 + m)] - taken[:, EP:]
            else:
                for n in range(5):
                    private[m, n, rows, :] = private[m, n, rows, :] - taken[:, 128 * n:128 * n + 128]

    def product(first, end):
        lanes = slice(128 * first, 128 * end)
        high = left_all[:, lanes]
        left = jnp.concatenate([high, left_all[:, EP + 128 * first:EP + 128 * end], high], axis=1)
        for n0, n1 in ((0, 256), (256, 512), (512, 640), (640, 896), (896, 1152), (1152, 1280)):
            high, low = halves(front[lanes, EP + n0:EP + n1])
            taken = mm(left, jnp.concatenate([high, high, low], axis=0))
            for n in range(n0, n1, 128):
                piece = taken[:, n - n0:n - n0 + 128]
                tile = slice(n, n + 128)
                if first:
                    front_out[:, tile] = front_out[:, tile] - piece[:E]
                elif n0 < EP:
                    front_out[:, tile] = private[0, n // 128, 0:E, :] - piece[:E]
                else:
                    front_out[:, tile] = -piece[:E]
                for w, who in enumerate((place, sibling)):
                    own_rows = piece[E + 40 * w:E + 40 * w + 40]
                    if first:
                        own_out[w, :, tile] = own_out[w, :, tile] - own_rows
                    elif n0 < EP:
                        own_out[w, :, tile] = -own_rows
                    else:
                        own_out[w, :, tile] = private[1, (n - EP) // 128, pl.ds(who, 40, stride=16), :] - own_rows

    def finished(j):
        for i in range(10):
            rows21[j, 128 * i:128 * i + 128, :] = front[128 * j:128 * j + 128, EP + 128 * i:EP + 128 * i + 128].T
        for i in range(j, 5):
            rows11[j, 128 * i:128 * i + 128, :] = front[128 * j:128 * j + 128, 128 * i:128 * i + 128].T
        for i in range(j):
            rows11[j, 128 * i:128 * i + 128, :] = jnp.zeros((128, 128), f32)
        some = [rows21[j, pl.ds(EP + who, 40, stride=16), :] for who in (place, sibling)]
        high, low = halves(jnp.concatenate([rows21[j, 0:E, :]] + some, axis=0))
        left_all[:, 128 * j:128 * j + 128] = high
        left_all[:, EP + 128 * j:EP + 128 * j + 128] = low
        if j == 2:
            product(0, 3)

    eliminate([front], finished=finished)
    product(3, 5)
    for w, who in enumerate((place, sibling)):
        spot1 = who % 8
        for n in range(0, EP, 128):
            rows_ref[w, 0, :, n:n + 128] = rows11[n // 128, pl.ds(spot1, 72, stride=8), :]
            rows_ref[w, 1, :, n:n + 128] = rows21[n // 128, pl.ds(spot1, 72, stride=8), :]
            rows_ref[w, 2, :, n:n + 128] = rows21[n // 128, pl.ds(EP + spot1, 72, stride=8), :]


def swap_kernel(front_ref, own_ref, rows_ref, front_in, own_in, rows_in, send, recv):
    greet((2,))
    pairs = [(rows_ref.at[1], rows_in), (own_ref.at[1], own_in)]
    for n in range(3):
        part = slice(192 * n, 192 * n + 192)
        pairs.append((front_ref.at[part, :], front_in.at[part, :]))
    copies = [
        pltpu.make_async_remote_copy(
            src, dst, send.at[n], recv.at[n], device_id=peer(2), device_id_type=MESH
        )
        for n, (src, dst) in enumerate(pairs)
    ]
    for copy in copies:
        copy.start()
    for copy in copies:
        copy.wait()


def top_kernel(
    early_ref, rows_ref, rows_in, front_ref, front_in, own_ref, own_in, out_ref, top_ref, front, rows11, own, stage
):
    place = group_place()
    core = place // 2 % 2
    here = core == place // 8
    for h in range(3):
        stage[h, 0:144, :] = early_ref[h]
        stage[h, 144:216, :] = jnp.where(here, rows_ref[0, h], rows_in[h])

    def finish(r):
        wide = min(128, 252 - r)
        for h in range(3):
            for n in range(0, E, 128):
                tall = min(128, E - n)
                out_ref[h, n:n + tall, r:r + wide] = stage[h, r:r + 128, n:n + 128].T[:tall, :wide]

    front[E:EP, :] = jnp.zeros((EP - E, WIDE), f32)
    own[...] = jnp.zeros(own.shape, f32)
    front[0:E, 0:EP] = front_ref[:, 0:EP] + front_in[:, 0:EP]
    for side, matrix, few in ((core, front_ref, own_ref.at[0]), (1 - core, front_in, own_in)):
        lanes = pl.ds(pl.multiple_of(EP * (1 + side), 128), EP)
        rows = pl.ds(pl.multiple_of(40 * side, 8), 40)
        front[0:E, lanes] = matrix[:, EP:]
        own[rows, 0:EP] = few[:, 0:EP]
        own[rows, lanes] = few[:, EP:]

    def finished(j):
        for i in range(j, 5):
            rows11[j, 128 * i:128 * i + 128, :] = front[128 * j:128 * j + 128, 128 * i:128 * i + 128].T
        for i in range(j):
            rows11[j, 128 * i:128 * i + 128, :] = jnp.zeros((128, 128), f32)
        if j == 1:
            finish(0)

    eliminate([front], own, finished)
    for n in range(0, EP, 128):
        stage[0, 216:252, n:n + 128] = rows11[n // 128, pl.ds(place, 36, stride=16), :]
    for h in range(2):
        stage[1 + h, 216:252, :] = own[40 * h:40 * h + 36, 0:EP]
        wide = jnp.concatenate([own[40 * h:40 * h + 40, EP:EP + E], own[40 * h:40 * h + 40, 2 * EP:2 * EP + E]], axis=1)
        for i in range(36):
            top_ref[36 * h + i] = wide[i:i + 1, :]
    finish(128)


VMEM = pl.BlockSpec(memory_space=pltpu.VMEM)
SMEM = pl.BlockSpec(memory_space=pltpu.SMEM)


FRONT = jax.ShapeDtypeStruct((E, 2 * EP), f32)


def groups(ids, raw, factors, last):
    return pl.pallas_call(
        groups_kernel,
        out_shape=(
            jax.ShapeDtypeStruct((3, 144, EP), f32),
            jax.ShapeDtypeStruct((2, 3, 72, EP), f32),
            FRONT,
            jax.ShapeDtypeStruct((2, 40, 2 * EP), f32),
        ),
        in_specs=[SMEM, VMEM, VMEM, VMEM],
        out_specs=(VMEM,) * 4,
        scratch_shapes=[
            pltpu.VMEM((EP, WIDE), f32),
            pltpu.VMEM((2, 5, EP, 128), f32),
            pltpu.VMEM((NB, BW, 2 * EP), f32),
            pltpu.VMEM((NB, BW, 2 * EP), bf16),
            pltpu.VMEM((NB, BW, 2 * EP), bf16),
            pltpu.VMEM((5, 2 * EP, 128), f32),
            pltpu.VMEM((5, EP, 128), f32),
            pltpu.VMEM((E + 80, 2 * EP), bf16),
            pltpu.VMEM((32, BW, 128), f32),
            pltpu.VMEM((3 * NB, 3 * BW, BW), bf16),
        ],
        compiler_params=pltpu.CompilerParams(vmem_limit_bytes=32 * 2**20),
    )(ids, raw, factors, last)


def swap(front, own, rows):
    dma = pltpu.SemaphoreType.DMA
    return pl.pallas_call(
        swap_kernel,
        out_shape=(
            FRONT,
            jax.ShapeDtypeStruct((40, 2 * EP), f32),
            jax.ShapeDtypeStruct((3, 72, EP), f32),
        ),
        in_specs=[VMEM] * 3,
        out_specs=(VMEM,) * 3,
        scratch_shapes=[dma((5,)), dma((5,))],
        compiler_params=pltpu.CompilerParams(
            collective_id=1, has_side_effects=True, vmem_limit_bytes=4 * 2**20
        ),
    )(front, own, rows)


def top(early, rows, rows_in, front, front_in, own, own_in):
    return pl.pallas_call(
        top_kernel,
        out_shape=(jax.ShapeDtypeStruct((3, E, 252), f32), jax.ShapeDtypeStruct((72, 1, 2 * E), f32)),
        in_specs=[VMEM] * 7,
        out_specs=(VMEM, VMEM),
        scratch_shapes=[
            pltpu.VMEM((EP, WIDE), f32),
            pltpu.VMEM((5, EP, 128), f32),
            pltpu.VMEM((80, WIDE), f32),
            pltpu.VMEM((3, 256, EP), f32),
        ],
        compiler_params=pltpu.CompilerParams(vmem_limit_bytes=20 * 2**20),
    )(early, rows, rows_in, front, front_in, own, own_in)


def exchange(cameras, landmarks, tiles):
    dma = pltpu.SemaphoreType.DMA
    return pl.pallas_call(
        exchange_kernel,
        out_shape=(
            jax.ShapeDtypeStruct((PEERS, 4, BW, 128), f32),
            jax.ShapeDtypeStruct((PEERS, BW, 128), f32),
            jax.ShapeDtypeStruct((4, BW // 2, 128), f32),
            jax.ShapeDtypeStruct((PEERS, 8, 128), jnp.int32),
        ),
        in_specs=[SMEM, SMEM, VMEM],
        out_specs=(VMEM, VMEM, VMEM, VMEM),
        scratch_shapes=[
            pltpu.VMEM((2, BW, 128), f32),
            pltpu.VMEM((4, 2, BW, 128), f32),
            pltpu.VMEM((BW, 128), f32),
            pltpu.VMEM((BW // 2, 128), f32),
            dma((4,)), dma((4,)), dma((PEERS,)), dma((PEERS,)),
            dma((9,)), dma((9,)), dma((10,)), dma((10,)),
            dma((PEERS,)), dma((PEERS,)), dma((PEERS,)), dma((3,)), dma((3,)),
        ],
        compiler_params=pltpu.CompilerParams(
            collective_id=0, has_side_effects=True, vmem_limit_bytes=8 * 2**20
        ),
    )(cameras, landmarks, tiles)


def local(jacobian, camera_block, landmark_block):
    blocks = jacobian[0]
    tiles = jnp.einsum("nrc,nrd->ncd", blocks, blocks, preferred_element_type=f32)
    raw, factors, last, ids = exchange(camera_block, landmark_block, tiles)
    early, rows, front, own = groups(ids, raw, factors, last)
    front_in, own_in, rows_in = swap(front, own, rows)
    factor_rows, top_rows = top(early, rows, rows_in, front, front_in, own, own_in)
    return factor_rows.transpose(0, 2, 1)[:, None], top_rows.reshape(2, 36, 1, 2 * E).transpose(0, 2, 1, 3)


def solution(mesh):
    placed = (P("sub", "lm", None, None), P("sub", "lm"), P("sub", "lm"))
    return jax.shard_map(
        local,
        mesh=mesh,
        in_specs=placed,
        out_specs=(P(None, ("sub", "lm"), None, None), P(None, ("sub", "lm"), None, None)),
        check_vma=False,
    )
```
